128 devices in a mesh: img: 16 (over y, z_lo, core), txt: 8 (over x, z_hi).
Axes of the slice: x: 4, y: 4, z: 4 (z_hi: 2, z_lo: 2; z = z_hi * 2 + z_lo), core: 2. Of those that a mesh axis runs over, the one named last changes fastest.
Arguments:
- image_embed: float32 [16384, 1152], P(('img', 'txt')), may hold values from -0.18 to 0.18
- text_embed: float32 [16384, 1152], P(('txt', 'img')), may hold values from -0.18 to 0.18
- log_scale: float32 [], replicated, may hold values from 1.5 to 2.5
- logit_bias: float32 [], replicated, may hold values from -4 to -2
Outputs:
- loss_mean: float32 [], replicated
- image_grad: float32 [16384, 1152], P(('img', 'txt'))
- text_grad: float32 [16384, 1152], P(('txt', 'img'))
- scale_grad: float32 [], replicated
- bias_grad: float32 [], replicated
The draws below stay inside these ranges and needn't reach their ends.
All inputs are finite; a program needn't handle non-finite values.
Results may differ from the reference program's by a relative error of at most 0.001.
The reference program's roundings to bfloat16 on the way (of `weight`) count: a program that leaves them out, or rounds other values in their place, can miss the bound.
Values may be sent and summed in bfloat16 or wider, within the bound.
No kernel may reach another device: no remote copies, remote signals or barrier semaphores. Data moves between devices by JAX's collectives and lax.ppermute only.
A program may use at most 128 MiB of HBM per device.

```python
import jax
import jax.numpy as jnp
from jax import lax

D = 1152
BATCH = 16384


def steps_of(stream_key, dims, split, least, top_value):
    def one(position, shards_of):
        draws = jax.random.uniform(jax.random.fold_in(jax.random.fold_in(stream_key, 6), position), (shards_of,), jnp.float32, least / len(split), top_value / len(split))
        return jnp.repeat(jnp.exp(draws), dims[position] // shards_of).reshape((-1,) + (1,) * (len(dims) - position - 1))

    gain = one(*split[0])
    for cut in split[1:]:
        gain = gain * one(*cut)
    return gain


def gaussian(stream_key, dims, scale, most, pieces=(), held_as=jnp.bfloat16):
    entries = jax.random.normal(stream_key, dims, jnp.float32) * scale
    if len(pieces) > 0:
        entries = steps_of(stream_key, dims, pieces, -0.22, 0.18) * entries
    return jnp.clip(entries, min=-most, max=most).astype(held_as)


def setup_inputs(seed: int = 0) -> dict:
    keys = jax.random.split(jax.random.key(seed), 5)
    image_embed = gaussian(keys[0], (BATCH, D), 0.03, 0.18, ((0, 128),), jnp.float32)
    text_embed = gaussian(keys[1], (BATCH, D), 0.03, 0.18, ((0, 128),), jnp.float32)
    log_scale = jnp.clip(jax.random.uniform(keys[2], (), jnp.float32, 1.5, 2.5), 1.5, 2.5)
    logit_bias = jnp.clip(jax.random.uniform(keys[3], (), jnp.float32, -4.0, -2.0), -4.0, -2.0)
    return {"image_embed": image_embed, "text_embed": text_embed, "log_scale": log_scale, "logit_bias": logit_bias}


def normalize(embed):
    norm = jnp.sqrt(lax.optimization_barrier(jnp.sum(embed * embed, axis=1, keepdims=True)) + 1e-06)
    return (embed / norm, norm)

def unnormalize(hat, norm, pull):
    return (pull - hat * lax.optimization_barrier(jnp.sum(hat * pull, axis=1, keepdims=True))) / norm

def reference(image_embed, text_embed, log_scale, logit_bias):
    image_hat, image_norm = normalize(image_embed)
    text_hat, text_norm = normalize(text_embed)
    image_low = image_hat.astype(jnp.bfloat16)
    text_low = text_hat.astype(jnp.bfloat16)
    scale = jnp.exp(log_scale)
    block = min(1024, BATCH)
    count = BATCH // block
    columns = jnp.arange(BATCH, dtype=jnp.int32)

    def step(carry, index):
        total, scale_sum, bias_sum, text_pull = carry
        start = (index * block).astype(jnp.int32)
        rows = lax.dynamic_slice_in_dim(image_low, start, block, 0)
        similar = jnp.dot(rows, text_low.T, preferred_element_type=jnp.float32)
        logit = scale * similar + logit_bias
        row_ids = start + jnp.arange(block, dtype=jnp.int32)
        sign = jnp.where(row_ids[:, None] == columns[None, :], 1.0, -1.0).astype(jnp.float32)
        total = total + jnp.sum(jax.nn.softplus(-sign * logit))
        slope = -sign * jax.nn.sigmoid(-sign * logit)
        scale_sum = scale_sum + jnp.sum(slope * scale * similar)
        bias_sum = bias_sum + jnp.sum(slope)
        weight = (scale * slope).astype(jnp.bfloat16)
        image_pull = jnp.dot(weight, text_low, preferred_element_type=jnp.float32)
        text_pull = text_pull + jnp.dot(weight.T, rows, preferred_element_type=jnp.float32)
        return ((total, scale_sum, bias_sum, text_pull), image_pull)
    zero = jnp.zeros((), jnp.float32)
    init = (zero, zero, zero, jnp.zeros((BATCH, D), jnp.float32))
    (total, scale_sum, bias_sum, text_pull), image_pull = lax.scan(step, init, jnp.arange(count, dtype=jnp.int32))
    image_pull = image_pull.reshape(BATCH, D)
    pairs = jnp.float32(BATCH) * jnp.float32(BATCH)
    image_grad = unnormalize(image_hat, image_norm, image_pull)
    text_grad = unnormalize(text_hat, text_norm, text_pull)
    return (total / pairs, image_grad, text_grad, scale_sum / pairs, bias_sum / pairs)
```

```python
import jax
import jax.numpy as jnp
from jax import lax
from jax.experimental import pallas as pl
from jax.experimental.pallas import tpu as pltpu
from jax.sharding import PartitionSpec as P

BF = jnp.bfloat16
F32 = jnp.float32
LOG2E = 1.4426950408889634
ANY = pl.BlockSpec(memory_space=pl.ANY)
VM = pl.BlockSpec(memory_space=pltpu.VMEM)
SM = pl.BlockSpec(memory_space=pltpu.SMEM)
CHUNK = 512
STRIP = 64


def sds(shape, dtype):
    return jax.ShapeDtypeStruct(shape, dtype)


def params():
    return pltpu.CompilerParams(vmem_limit_bytes=56 * 1024 * 1024)


def encode(x):
    sq = x * x
    return (sq * sq * sq * x).astype(BF)


def decode(code):
    y = code.astype(F32)
    size = jnp.abs(y)
    root = jnp.exp2(jnp.log2(jnp.maximum(size, 1.2e-38)) * (1.0 / 7.0))
    root = jnp.where(size < 1.2e-38, 0.0, root)
    return jnp.where(y < 0, -root, root)


def normalize_kernel(a_ref, b_ref, a_out, b_out):
    for src, dst in ((a_ref, a_out), (b_ref, b_out)):
        x = src[...]
        norm = jnp.sqrt(jnp.sum(x * x, axis=1, keepdims=True) + 1e-06)
        dst[...] = (x / norm).astype(BF)


def normalize(a, b):
    return pl.pallas_call(
        normalize_kernel,
        out_shape=(sds(a.shape, BF), sds(b.shape, BF)),
        name="normalize",
    )(a, b)


def dot(a, b, dims):
    return lax.dot_general(a, b, (dims, ((), ())), preferred_element_type=F32)


def tile_kernel(ni, nt, rows, *refs):
    scal, diag = refs[0], refs[1]
    image_in, text_in = refs[2 : 2 + ni], refs[2 + ni : 2 + ni + nt]
    refs = refs[2 + ni + nt :]
    image_own, text_own = refs[0], refs[1]
    image_code, text_code, sums = refs[2], refs[3], refs[4]
    xs, ts, sim, wgt, pull, tp, isem, tsem, osem = refs[5:]
    m = ni * rows
    n = nt * rows
    copies_i = [
        pltpu.make_async_copy(r, xs.at[pl.ds(k * rows, rows)], isem.at[k]) for k, r in enumerate(image_in)
    ]
    copies_t = [
        pltpu.make_async_copy(r, ts.at[pl.ds(k * rows, rows)], tsem.at[k]) for k, r in enumerate(text_in)
    ]
    for c in copies_i + copies_t:
        c.start()
    for c in copies_i + copies_t:
        c.wait()
    scale = jnp.exp(jnp.full((1, 1), scal[0], F32))
    bias = scal[1]
    mult = scale * LOG2E
    shift = bias * LOG2E
    chunks = n // CHUNK
    half = chunks // 2
    per = CHUNK // rows
    sums[...] = jnp.zeros_like(sums)

    def step(c, carry):
        tc = ts[pl.ds(pl.multiple_of(c * CHUNK, CHUNK), CHUNK), :]
        sim[...] = dot(xs[...], tc, ((1,), (1,)))

        def strip(r, acc):
            loss, slope_sum, scale_sum = acc
            at = pl.ds(pl.multiple_of(r * STRIP, STRIP), STRIP)
            s = sim[at, :]
            e = jnp.exp2(s * mult + shift)
            u = e + 1.0
            r0 = pl.reciprocal(u, approx=True)
            sig = e * (r0 * (2.0 - u * r0))
            wgt[at, :] = (sig * scale).astype(BF)
            prod = u[0:8]
            for k in range(1, STRIP // 8):
                prod = prod * u[8 * k : 8 * k + 8]
            loss = loss + jnp.log(prod)
            ss = sig * s
            a, b = sig[0:8], ss[0:8]
            for k in range(1, STRIP // 8):
                a = a + sig[8 * k : 8 * k + 8]
                b = b + ss[8 * k : 8 * k + 8]
            return loss, slope_sum + a, scale_sum + b

        zero = jnp.zeros((8, CHUNK), F32)
        loss, slope_sum, scale_sum = lax.fori_loop(0, m // STRIP, strip, (zero, zero, zero))
        sums[0:8] += loss
        sums[8:16] += slope_sum
        sums[16:24] += scale_sum
        for b in range(ni):
            place = diag[b] - c * per

            @pl.when(jnp.logical_and(place >= 0, place < per))
            def _(b=b, place=place):
                at = (pl.ds(b * rows, rows), pl.ds(pl.multiple_of(place * rows, rows), rows))
                s = sim[at]
                eye = lax.broadcasted_iota(jnp.int32, s.shape, 0) == lax.broadcasted_iota(jnp.int32, s.shape, 1)
                z = scale * s + bias
                w = (-scale / (1.0 + jnp.exp(z))).astype(BF)
                wgt[at] = jnp.where(eye, w.astype(F32), wgt[at].astype(F32)).astype(BF)
                z = jnp.where(eye, z, 0.0)
                sd = jnp.where(eye, s, 0.0)
                one = jnp.where(eye, 1.0, 0.0)
                for row, v in ((0, z), (8, one), (16, sd)):
                    total = v[0:8]
                    for k in range(1, rows // 8):
                        total = total + v[8 * k : 8 * k + 8]
                    sums[row : row + 8, 0:rows] -= total

        tp[...] = dot(wgt[...], xs[...], ((0,), (0,)))

        @pl.when(c < half)
        def _():
            text_own[pl.ds(pl.multiple_of(c * CHUNK, CHUNK), CHUNK), :] = tp[...]

        @pl.when(c >= half)
        def _():
            text_code[pl.ds(pl.multiple_of((c - half) * CHUNK, CHUNK), CHUNK), :] = encode(tp[...])

        part = dot(wgt[...], tc, ((1,), (0,)))

        @pl.when(c == 0)
        def _():
            pull[...] = part

        @pl.when(c > 0)
        def _():
            pull[...] += part

        return carry

    lax.fori_loop(0, chunks, step, 0)
    copies = []
    for z in range(2):
        image_own[z * rows : (z + 1) * rows] = pull[4 * z * rows : (4 * z + 1) * rows]
        for k in range(1, 4):
            image_code[k - 1, z * rows : (z + 1) * rows] = encode(
                pull[(4 * z + k) * rows : (4 * z + k + 1) * rows]
            )


def tile(scal, diag, images, texts):
    rows, d = images[0].shape
    ni, nt = len(images), len(texts)
    m, n = ni * rows, nt * rows

    def body(*refs):
        k = 2 + ni + nt
        ins, rest = refs[:k], refs[k:]
        image_own, text_own, c1, c2, c3, text_code, sums = rest[:7]

        class Codes:
            def __setitem__(self, at, value):
                (c1, c2, c3)[at[0]][at[1], :] = value

        tile_kernel(ni, nt, rows, *ins, image_own, text_own, Codes(), text_code, sums, *rest[7:])

    return pl.pallas_call(
        body,
        in_specs=[SM, SM] + [ANY] * (ni + nt),
        out_specs=[VM] * 7,
        out_shape=(
            sds((2 * rows, d), F32),
            sds((n // 2, d), F32),
            sds((2 * rows, d), BF),
            sds((2 * rows, d), BF),
            sds((2 * rows, d), BF),
            sds((n // 2, d), BF),
            sds((24, CHUNK), F32),
        ),
        scratch_shapes=[
            pltpu.VMEM((m, d), BF),
            pltpu.VMEM((n, d), BF),
            pltpu.VMEM((m, CHUNK), F32),
            pltpu.VMEM((m, CHUNK), BF),
            pltpu.VMEM((m, d), F32),
            pltpu.VMEM((CHUNK, d), F32),
            pltpu.SemaphoreType.DMA((ni,)),
            pltpu.SemaphoreType.DMA((nt,)),
            pltpu.SemaphoreType.DMA((4,)),
        ],
        compiler_params=params(),
        cost_estimate=pl.CostEstimate(
            flops=6 * m * n * d, bytes_accessed=(m + n) * d * 8, transcendentals=3 * m * n
        ),
        name="tile",
    )(scal, diag, *images, *texts)


def fold_core_kernel(own_ref, code_ref, own_out, c1, c2, c3):
    rows = own_out.shape[0] // 2
    for z in range(2):
        for k in range(4):
            at = pl.ds((4 * z + k) * rows, rows)
            total = own_ref[at, :] + decode(code_ref[at, :])
            to = pl.ds(z * rows, rows)
            if k == 0:
                own_out[to, :] = total
            else:
                (c1, c2, c3)[k - 1][to, :] = encode(total)


def fold_core(own, code):
    rows, d = own.shape[0] // 4, own.shape[1]
    return pl.pallas_call(
        fold_core_kernel,
        out_shape=(sds((rows, d), F32),) + (sds((rows, d), BF),) * 3,
        compiler_params=params(),
        name="fold_core",
    )(own, code)


def fold_ring_kernel(own_ref, c1, c2, c3, own_out, code_out):
    rows = own_out.shape[0]
    for z in range(2):
        at = pl.ds(z * rows, rows)
        total = own_ref[at, :]
        for c in (c1, c2, c3):
            total = total + decode(c[at, :])
        if z == 0:
            own_out[...] = total
        else:
            code_out[...] = encode(total)


def fold_ring(own, codes):
    rows, d = own.shape[0] // 2, own.shape[1]
    return pl.pallas_call(
        fold_ring_kernel,
        out_shape=(sds((rows, d), F32), sds((rows, d), BF)),
        compiler_params=params(),
        name="fold_ring",
    )(own, *codes)


def finish_kernel(x_ref, own_ref, code_ref, out_ref):
    x = x_ref[...]
    norm = jnp.sqrt(jnp.sum(x * x, axis=1, keepdims=True) + 1e-06)
    hat = x / norm
    pull = own_ref[...] + decode(code_ref[...])
    out_ref[...] = (pull - hat * jnp.sum(hat * pull, axis=1, keepdims=True)) / norm


def finish(x, own, code):
    return pl.pallas_call(
        finish_kernel, out_shape=sds(x.shape, F32), compiler_params=params(), name="finish"
    )(x, own, code)


def img_index(y, z, c):
    return (y % 4) * 4 + (z % 2) * 2 + c % 2


def perm_x(shift):
    return [(i, ((i // 2 + shift) % 4) * 2 + i % 2) for i in range(8)]


def perm_y(shift):
    return [(i, img_index(i // 4 + shift, i // 2, i)) for i in range(16)]


PERM_ZHI = [(i, i ^ 1) for i in range(8)]
PERM_ZLO = [(i, i ^ 2) for i in range(16)]
PERM_CORE = [(i, i ^ 1) for i in range(16)]


def local(image_embed, text_embed, log_scale, logit_bias):
    image_low, text_low = normalize(image_embed, text_embed)
    send = lax.ppermute
    image_z = send(image_low, "txt", PERM_ZHI)
    text_z = send(text_low, "img", PERM_ZLO)
    images = [image_low] + [send(image_low, "txt", perm_x(k)) for k in (1, 2, 3)]
    texts = [text_low] + [send(text_low, "img", perm_y(k)) for k in (1, 2, 3)]
    images += [image_z] + [send(image_z, "txt", perm_x(k)) for k in (1, 2, 3)]
    texts += [text_z] + [send(text_z, "img", perm_y(k)) for k in (1, 2, 3)]
    texts += [send(t, "img", PERM_CORE) for t in texts]

    i, t = lax.axis_index("img"), lax.axis_index("txt")
    b = jnp.arange(8, dtype=jnp.int32)
    g = 8 * i + (((t // 2 - b % 4) % 4) * 2 + ((t % 2) ^ (b // 4)))
    o = g % 16
    place = ((i % 2) ^ (o % 2)) * 8 + (((i // 2) % 2) ^ ((o // 2) % 2)) * 4 + (i // 4 - o // 4) % 4
    diag = jnp.where(g // 16 == t, place, -1).astype(jnp.int32)
    scal = jnp.stack([log_scale, logit_bias])

    image_own, text_own, i1, i2, i3, text_code, sums = tile(scal, diag, images, texts)

    text_code = send(text_code, "img", PERM_CORE)
    codes = [send(c, "txt", perm_x(-k)) for k, c in ((1, i1), (2, i2), (3, i3))]
    text_own, t1, t2, t3 = fold_core(text_own, text_code)
    tcodes = [send(c, "img", perm_y(-k)) for k, c in ((1, t1), (2, t2), (3, t3))]

    v = jnp.sum(sums.reshape(3, 8, -1), axis=(1, 2))
    v = jnp.broadcast_to(v[:, None], (3, 128))
    v = (v + send(v, "txt", perm_x(2))) + (send(v, "txt", perm_x(1)) + send(v, "txt", perm_x(3)))
    v = (v + send(v, "img", perm_y(2))) + (send(v, "img", perm_y(1)) + send(v, "img", perm_y(3)))
    v = v + send(v, "txt", PERM_ZHI)
    v = v + send(v, "img", PERM_ZLO)
    v = v + send(v, "img", PERM_CORE)

    image_own, image_code = fold_ring(image_own, codes)
    image_code = send(image_code, "txt", PERM_ZHI)
    text_own, text_code = fold_ring(text_own, tcodes)
    text_code = send(text_code, "img", PERM_ZLO)
    image_grad = finish(image_embed, image_own, image_code)
    text_grad = finish(text_embed, text_own, text_code)
    pairs = F32(16384.0 * 16384.0)
    scale = jnp.exp(log_scale)
    return (v[0, 0] / pairs, image_grad, text_grad, v[2, 0] * scale / pairs, v[1, 0] / pairs)


def solution(mesh):
    placed = (P(("img", "txt"), None), P(("txt", "img"), None), P(), P())
    return jax.shard_map(
        local,
        mesh=mesh,
        in_specs=placed,
        out_specs=(P(), P(("img", "txt"), None), P(("txt", "img"), None), P(), P()),
        check_vma=False,
    )
```

```python
import jax
import jax.numpy as jnp
from jax import lax
from jax.experimental import pallas as pl
from jax.experimental.pallas import tpu as pltpu
from jax.sharding import PartitionSpec as P

BF = jnp.bfloat16
F32 = jnp.float32
LOG2E = 1.4426950408889634
ANY = pl.BlockSpec(memory_space=pl.ANY)
VM = pl.BlockSpec(memory_space=pltpu.VMEM)
SM = pl.BlockSpec(memory_space=pltpu.SMEM)
STRIP = 256
PIECE = 512
SLOT = {2: 0, 1: 1, 3: 2, 0: 3}


def sds(shape, dtype):
    return jax.ShapeDtypeStruct(shape, dtype)


def params():
    return pltpu.CompilerParams(vmem_limit_bytes=56 * 1024 * 1024)


def encode(x):
    sq = x * x
    return (sq * sq * sq * x).astype(BF)


def decode(code):
    y = code.astype(F32)
    return y * jnp.exp2(jnp.log2(jnp.maximum(jnp.abs(y), 1.2e-38)) * (-6.0 / 7.0))


def dot(a, b, dims):
    return lax.dot_general(a, b, (dims, ((), ())), preferred_element_type=F32)


def normalize_kernel(a_ref, b_ref, a_out, b_out):
    for src, dst in ((a_ref, a_out), (b_ref, b_out)):
        x = src[...]
        norm = jnp.sqrt(jnp.sum(x * x, axis=1, keepdims=True) + 1e-06)
        dst[...] = (x / norm).astype(BF)


def normalize(a, b):
    return pl.pallas_call(
        normalize_kernel, out_shape=(sds(a.shape, BF), sds(b.shape, BF)), name="normalize"
    )(a, b)


def loads(refs, dest, sems, base=0):
    out, at = [], base
    for n, r in enumerate(refs):
        out.append(pltpu.make_async_copy(r, dest.at[pl.ds(at, r.shape[0])], sems.at[n]))
        at += r.shape[0]
    return out


def start(copies):
    for c in copies:
        c.start()


def wait(copies):
    for c in copies:
        c.wait()


def scores(scal, diag, first, xs, ts, sim, wgt, sums):
    m, n, rows = xs.shape[0], ts.shape[0], xs.shape[0] // 8
    scale = jnp.exp(jnp.full((1, 1), scal[0], F32))
    bias = scal[1]
    mult = scale * LOG2E
    shift = bias * LOG2E
    pieces = [(r, c) for r in range(0, m, STRIP) for c in range(0, n, PIECE)]

    def score(r, c):
        sim[r : r + STRIP, c : c + PIECE] = dot(xs[r : r + STRIP, :], ts[c : c + PIECE, :], ((1,), (1,)))

    acc = [jnp.zeros((8, PIECE), F32) for _ in range(3)]
    score(*pieces[0])
    for p, (r, c) in enumerate(pieces):
        if p + 1 < len(pieces):
            score(*pieces[p + 1])
        prod = None
        for i in range(0, STRIP, 16):
            s = sim[r + i : r + i + 16, c : c + PIECE]
            e = jnp.exp2(s * mult + shift)
            u = e + 1.0
            r0 = pl.reciprocal(u, approx=True)
            sig = e * (r0 * (2.0 - u * r0))
            wgt[r + i : r + i + 16, c : c + PIECE] = (sig * scale).astype(BF)
            both = u[0:8] * u[8:16]
            prod = both if prod is None else prod * both
            if i % 64 == 48:
                acc[0] = acc[0] + jnp.log(prod)
                prod = None
            ss = sig * s
            acc[1] = acc[1] + (sig[0:8] + sig[8:16])
            acc[2] = acc[2] + (ss[0:8] + ss[8:16])
    for k in range(3):
        sums[8 * k : 8 * k + 8] = acc[k]

    for b in range(8):
        place = diag[b] - first

        @pl.when(jnp.logical_and(place >= 0, place < n // rows))
        def _(b=b, place=place):
            at = (pl.ds(b * rows, rows), pl.ds(pl.multiple_of(place * rows, rows), rows))
            s = sim[at]
            eye = lax.broadcasted_iota(jnp.int32, s.shape, 0) == lax.broadcasted_iota(jnp.int32, s.shape, 1)
            z = scale * s + bias
            w = -scale / (1.0 + jnp.exp(z))
            wgt[at] = jnp.where(eye, w, wgt[at].astype(F32)).astype(BF)
            z = jnp.where(eye, z, 0.0)
            sd = jnp.where(eye, s, 0.0)
            one = jnp.where(eye, 1.0, 0.0)
            for row, v in ((0, z), (8, one), (16, sd)):
                total = v[0:8]
                for k in range(1, rows // 8):
                    total = total + v[8 * k : 8 * k + 8]
                sums[row : row + 8, 0:rows] -= total


def first_kernel(ni, nt, scal, diag, *refs):
    images, texts = refs[:ni], refs[ni : ni + nt]
    w_out, tp_out, sums, xs, ts, sim, wgt, tp, isem, tsem, osem = refs[ni + nt :]
    copies = loads(texts, ts, tsem) + loads(images, xs, isem)
    start(copies)
    wait(copies)
    scores(scal, diag, 0, xs, ts, sim, wgt, sums)
    w_copy = pltpu.make_async_copy(wgt, w_out, osem.at[0])
    w_copy.start()
    outs = [w_copy]
    for n, r in enumerate(range(0, ts.shape[0], STRIP)):
        tp[r : r + STRIP, :] = dot(wgt[:, r : r + STRIP], xs[...], ((0,), (0,)))
        c = pltpu.make_async_copy(tp.at[pl.ds(r, STRIP)], tp_out.at[pl.ds(r, STRIP)], osem.at[1 + n])
        c.start()
        outs.append(c)
    wait(outs)


def first(scal, diag, images, texts, m, n, d):
    ni, nt = len(images), len(texts)
    return pl.pallas_call(
        lambda *refs: first_kernel(ni, nt, *refs),
        in_specs=[SM, SM] + [ANY] * (ni + nt),
        out_specs=[ANY, ANY, VM],
        out_shape=(sds((m, n), BF), sds((n, d), F32), sds((24, PIECE), F32)),
        scratch_shapes=[
            pltpu.VMEM((m, d), BF),
            pltpu.VMEM((n, d), BF),
            pltpu.VMEM((m, n), F32),
            pltpu.VMEM((m, n), BF),
            pltpu.VMEM((n, d), F32),
            pltpu.SemaphoreType.DMA((ni,)),
            pltpu.SemaphoreType.DMA((nt,)),
            pltpu.SemaphoreType.DMA((1 + n // STRIP,)),
        ],
        compiler_params=params(),
        cost_estimate=pl.CostEstimate(
            flops=4 * m * n * d, bytes_accessed=(m + n) * d * 4, transcendentals=3 * m * n
        ),
        name="other_half",
    )(scal, diag, *images, *texts)


def put_groups(pulls, rows, far_a, far_b, k1, k3, own):
    far = pulls(SLOT[2])
    far_a[...] = encode(far[:rows])
    far_b[...] = encode(far[rows:])
    for k, ref in ((1, k1), (3, k3), (0, own)):
        ref[...] = pulls(SLOT[k])


def second_kernel(ni, nt, scal, diag, *refs):
    images, own, other = refs[:ni], refs[ni : ni + nt], refs[ni + nt : ni + 2 * nt]
    w_in = refs[ni + 2 * nt]
    w_out, far_a, far_b, k1, k3, k0, sums = refs[ni + 2 * nt + 1 : ni + 2 * nt + 8]
    xs, ts, to, sim, wgt, wo, isem, tsem, osem, wsem = refs[ni + 2 * nt + 8 :]
    now = loads(own, ts, tsem) + loads(images, xs, isem)
    later = loads(other, to, osem) + [pltpu.make_async_copy(w_in, wo, wsem.at[0])]
    start(now)
    start(later)
    wait(now)
    scores(scal, diag, 8, xs, ts, sim, wgt, sums)
    w_copy = pltpu.make_async_copy(wgt, w_out, wsem.at[1])
    w_copy.start()
    wait(later)

    def pulls(slot):
        at = slice(slot * STRIP, (slot + 1) * STRIP)
        return dot(wgt[at, :], ts[...], ((1,), (0,))) + dot(wo[at, :], to[...], ((1,), (0,)))

    put_groups(pulls, xs.shape[0] // 8, far_a, far_b, k1, k3, k0)
    w_copy.wait()


def group_shapes(rows, d):
    return (sds((rows, d), BF),) * 2 + (sds((2 * rows, d), F32),) * 3


def second(scal, diag, images, own, other, w_other, n, d):
    ni, nt = len(images), len(own)
    m = w_other.shape[0]
    return pl.pallas_call(
        lambda *refs: second_kernel(ni, nt, *refs),
        in_specs=[SM, SM] + [ANY] * (ni + 2 * nt + 1),
        out_specs=[ANY] + [VM] * 6,
        out_shape=(sds((m, n), BF),) + group_shapes(m // 8, d) + (sds((24, PIECE), F32),),
        scratch_shapes=[
            pltpu.VMEM((m, d), BF),
            pltpu.VMEM((n, d), BF),
            pltpu.VMEM((n, d), BF),
            pltpu.VMEM((m, n), F32),
            pltpu.VMEM((m, n), BF),
            pltpu.VMEM((m, n), BF),
            pltpu.SemaphoreType.DMA((ni,)),
            pltpu.SemaphoreType.DMA((nt,)),
            pltpu.SemaphoreType.DMA((nt,)),
            pltpu.SemaphoreType.DMA((2,)),
        ],
        compiler_params=params(),
        cost_estimate=pl.CostEstimate(
            flops=6 * m * n * d, bytes_accessed=(m + 2 * n) * d * 4, transcendentals=3 * m * n
        ),
        name="own_half",
    )(scal, diag, *images, *own, *other, w_other)


def third_kernel(ni, *refs):
    images, w_in, tp_in = refs[:ni], refs[ni], refs[ni + 1]
    far_a, far_b, k1, k3, k0, xs, wgt, tp, isem, wsem = refs[ni + 2 :]
    copies = loads(images, xs, isem) + [pltpu.make_async_copy(w_in, wgt, wsem.at[0])]
    later = pltpu.make_async_copy(tp_in, tp, wsem.at[1])
    start(copies)
    later.start()
    wait(copies)
    later.wait()

    def pulls(slot):
        at = slice(slot * STRIP, (slot + 1) * STRIP)
        return dot(wgt[:, at], xs[...], ((0,), (0,))) + tp[at, :]

    put_groups(pulls, wgt.shape[1] // 8, far_a, far_b, k1, k3, k0)


def third(images, w_own, tp):
    ni = len(images)
    (m, n), d = w_own.shape, tp.shape[1]
    return pl.pallas_call(
        lambda *refs: third_kernel(ni, *refs),
        in_specs=[ANY] * (ni + 2),
        out_specs=[VM] * 5,
        out_shape=group_shapes(n // 8, d),
        scratch_shapes=[
            pltpu.VMEM((m, d), BF),
            pltpu.VMEM((m, n), BF),
            pltpu.VMEM((n, d), F32),
            pltpu.SemaphoreType.DMA((ni,)),
            pltpu.SemaphoreType.DMA((2,)),
        ],
        compiler_params=params(),
        cost_estimate=pl.CostEstimate(
            flops=2 * m * n * d, bytes_accessed=(m + 2 * n) * d * 4, transcendentals=0
        ),
        name="own_text_pull",
    )(*images, w_own, tp)


def relay_kernel(k1, k3, via1, via3, c1, c3):
    rows = via1.shape[0]
    c1[:rows, :] = encode(k1[:rows, :])
    c1[rows:, :] = encode(k1[rows:, :] + decode(via1[...]))
    c3[:rows, :] = encode(k3[:rows, :] + decode(via3[...]))
    c3[rows:, :] = encode(k3[rows:, :])


def relay(k1, k3, via1, via3):
    return pl.pallas_call(
        relay_kernel, out_shape=(sds(k1.shape, BF),) * 2, compiler_params=params(), name="relay"
    )(k1, k3, via1, via3)


def partner_kernel(own, c1, c3, out):
    out[...] = encode(own[...] + decode(c1[...]) + decode(c3[...]))


def fold_partner(own, c1, c3):
    rows, d = own.shape[0] // 2, own.shape[1]
    half = pl.BlockSpec((rows, d), lambda i: (1, 0))
    return pl.pallas_call(
        partner_kernel,
        grid=(1,),
        in_specs=[half] * 3,
        out_specs=pl.BlockSpec((rows, d), lambda i: (0, 0)),
        out_shape=sds((rows, d), BF),
        compiler_params=params(),
        name="fold_partner",
    )(own, c1, c3)


def finish_kernel(x_ref, own, c1, c3, code_ref, out_ref):
    x = x_ref[...]
    norm = jnp.sqrt(jnp.sum(x * x, axis=1, keepdims=True) + 1e-06)
    hat = x / norm
    pull = own[...] + decode(c1[...]) + decode(c3[...]) + decode(code_ref[...])
    out_ref[...] = (pull - hat * jnp.sum(hat * pull, axis=1, keepdims=True)) / norm


def finish(x, own, c1, c3, code):
    whole = pl.BlockSpec(x.shape, lambda i: (0, 0))
    return pl.pallas_call(
        finish_kernel,
        grid=(1,),
        in_specs=[whole] * 5,
        out_specs=whole,
        out_shape=sds(x.shape, F32),
        compiler_params=params(),
        name="finish",
    )(x, own, c1, c3, code)


def img_index(y, z, c):
    return (y % 4) * 4 + (z % 2) * 2 + c % 2


def perm_x(shift):
    return [(i, ((i // 2 + shift) % 4) * 2 + i % 2) for i in range(8)]


def perm_y(shift):
    return [(i, img_index(i // 4 + shift, i // 2, i)) for i in range(16)]


PERM_ZHI = [(i, i ^ 1) for i in range(8)]
PERM_ZLO = [(i, i ^ 2) for i in range(16)]
PERM_CORE = [(i, i ^ 1) for i in range(16)]


def local(image_embed, text_embed, log_scale, logit_bias):
    send = lax.ppermute
    rows, d = image_embed.shape
    image_low, text_low = normalize(image_embed, text_embed)

    i0 = jnp.concatenate([image_low, send(image_low, "txt", PERM_ZHI)], 0)
    t0 = jnp.concatenate([text_low, send(text_low, "img", PERM_ZLO)], 0)
    i1, i3 = send(i0, "txt", perm_x(1)), send(i0, "txt", perm_x(-1))
    t1, t3 = send(t0, "img", perm_y(1)), send(t0, "img", perm_y(-1))
    i2 = [send(i1[:rows], "txt", perm_x(1)), send(i3[rows:], "txt", perm_x(-1))]
    t2 = [send(t1[:rows], "img", perm_y(1)), send(t3[rows:], "img", perm_y(-1))]
    images = i2 + [i1, i3, i0]
    own = t2 + [t1, t3, t0]
    other = [send(t, "img", PERM_CORE) for t in own]

    i, t = lax.axis_index("img"), lax.axis_index("txt")
    b = jnp.arange(8, dtype=jnp.int32)
    ring = jnp.array([2, 1, 3, 0], jnp.int32)
    g = 8 * i + ((t // 2 - ring[b // 2]) % 4) * 2 + ((t % 2) ^ (b % 2))
    o = g % 16
    slot = jnp.array([3, 1, 0, 2], jnp.int32)[(i // 4 - o // 4) % 4]
    mine = 1 - ((i % 2) ^ (o % 2))
    place = mine * 8 + slot * 2 + (((i // 2) % 2) ^ ((o // 2) % 2))
    diag = jnp.where(g // 16 == t, place, -1).astype(jnp.int32)
    scal = jnp.stack([log_scale, logit_bias])

    w_other, tp, sums = first(scal, diag, images, other, 8 * rows, 8 * rows, d)
    tp = send(tp, "img", PERM_CORE)
    w_own, ia, ib, k1, k3, k0, more = second(scal, diag, images, own, other, w_other, 8 * rows, d)

    ia, ib = send(ia, "txt", perm_x(1)), send(ib, "txt", perm_x(-1))
    ta, tb, q1, q3, q0 = third(images, w_own, tp)
    ta, tb = send(ta, "img", perm_y(1)), send(tb, "img", perm_y(-1))
    c1, c3 = relay(k1, k3, ib, ia)
    c1, c3 = send(c1, "txt", perm_x(-1)), send(c3, "txt", perm_x(1))
    e1, e3 = relay(q1, q3, tb, ta)
    e1, e3 = send(e1, "img", perm_y(-1)), send(e3, "img", perm_y(1))

    v = jnp.sum((sums + more).reshape(3, 8, -1), axis=(1, 2))
    v = jnp.broadcast_to(v[:, None], (3, 128))
    v = v + send(v, "img", PERM_CORE)
    for bit in (2, 4):
        v = v + send(v, "txt", [(i, i ^ bit) for i in range(8)])
    for bit in (4, 8):
        v = v + send(v, "img", [(i, i ^ bit) for i in range(16)])
    v = v + send(v, "txt", PERM_ZHI)
    v = v + send(v, "img", PERM_ZLO)

    image_code = send(fold_partner(k0, c1, c3), "txt", PERM_ZHI)
    text_code = send(fold_partner(q0, e1, e3), "img", PERM_ZLO)
    image_grad = finish(image_embed, k0, c1, c3, image_code)
    text_grad = finish(text_embed, q0, e1, e3, text_code)
    pairs = F32(128.0 * rows) * F32(128.0 * rows)
    scale = jnp.exp(log_scale)
    return (v[0, 0] / pairs, image_grad, text_grad, v[2, 0] * scale / pairs, v[1, 0] / pairs)


def solution(mesh):
    placed = (P(("img", "txt"), None), P(("txt", "img"), None), P(), P())
    return jax.shard_map(
        local,
        mesh=mesh,
        in_specs=placed,
        out_specs=(P(), P(("img", "txt"), None), P(("txt", "img"), None), P(), P()),
        check_vma=False,
    )
```

```python
import jax
import jax.numpy as jnp
from jax import lax
from jax.experimental import pallas as pl
from jax.experimental.pallas import tpu as pltpu
from jax.sharding import PartitionSpec as P

BF = jnp.bfloat16
F32 = jnp.float32
LOG2E = 1.4426950408889634
ANY = pl.BlockSpec(memory_space=pl.ANY)
VM = pl.BlockSpec(memory_space=pltpu.VMEM)
SM = pl.BlockSpec(memory_space=pltpu.SMEM)
STRIP = 256
TALL = 512
PIECE = 512
SLOT = {2: 0, 1: 1, 3: 2, 0: 3}


def sds(shape, dtype):
    return jax.ShapeDtypeStruct(shape, dtype)


def params():
    return pltpu.CompilerParams(vmem_limit_bytes=56 * 1024 * 1024)


def encode(x):
    sq = x * x
    return (sq * sq * sq * x).astype(BF)


def decode(code):
    y = code.astype(F32)
    return y * jnp.exp2(jnp.log2(jnp.maximum(jnp.abs(y), 1.2e-38)) * (-6.0 / 7.0))


def dot(a, b, dims):
    return lax.dot_general(a, b, (dims, ((), ())), preferred_element_type=F32)


def normalize_kernel(a_ref, b_ref, a_out, b_out):
    for src, dst in ((a_ref, a_out), (b_ref, b_out)):
        x = src[...]
        norm = jnp.sqrt(jnp.sum(x * x, axis=1, keepdims=True) + 1e-06)
        dst[...] = (x / norm).astype(BF)


def normalize(a, b):
    return pl.pallas_call(
        normalize_kernel, out_shape=(sds(a.shape, BF), sds(b.shape, BF)), name="normalize"
    )(a, b)


RING = (0, 1, 3, 2)


def block_copies(pair, dest, sems, base=0):
    out = {}
    for zz, ref in enumerate(pair):
        rows = ref.shape[0] // 4
        for j, k in enumerate(RING):
            at = base + (2 * SLOT[k] + zz) * rows
            out[at] = pltpu.make_async_copy(
                ref.at[pl.ds(j * rows, rows)], dest.at[pl.ds(at, rows)], sems.at[4 * zz + j]
            )
    return [out[at] for at in sorted(out)]


class Pending:
    def __init__(self, copies, rows):
        self.copies, self.rows, self.done = copies, rows, 0

    def start(self):
        for c in self.copies:
            c.start()

    def upto(self, row):
        while self.done < len(self.copies) and self.done * self.rows < row:
            self.copies[self.done].wait()
            self.done += 1


def scores(scal, diag, first, xs, ts, sim, wgt, sums, need):
    m, n, rows = xs.shape[0], ts.shape[0], xs.shape[0] // 8
    scale, bias, mult, shift = scal[0], scal[1], scal[2], scal[3]
    pieces = [(r, c) for r in range(0, m, TALL) for c in range(0, n, PIECE)]

    def score(r, c):
        need(r + TALL, c + PIECE)
        sim[r : r + TALL, c : c + PIECE] = dot(xs[r : r + TALL, :], ts[c : c + PIECE, :], ((1,), (1,)))

    acc = [jnp.zeros((8, PIECE), F32) for _ in range(3)]
    score(*pieces[0])
    for p, (r, c) in enumerate(pieces):
        if p + 1 < len(pieces):
            score(*pieces[p + 1])
        prod = None
        for i in range(0, TALL, 16):
            s = sim[r + i : r + i + 16, c : c + PIECE]
            e = jnp.exp2(s * mult + shift)
            u = e + 1.0
            r0 = pl.reciprocal(u, approx=True)
            sig = e * (r0 * (2.0 - u * r0))
            wgt[r + i : r + i + 16, c : c + PIECE] = (sig * scale).astype(BF)
            both = u[0:8] * u[8:16]
            prod = both if prod is None else prod * both
            if i % 64 == 48:
                acc[0] = acc[0] + jnp.log(prod)
                prod = None
            ss = sig * s
            acc[1] = acc[1] + (sig[0:8] + sig[8:16])
            acc[2] = acc[2] + (ss[0:8] + ss[8:16])
    for k in range(3):
        sums[8 * k : 8 * k + 8] = acc[k]

    for b in range(8):
        place = diag[b] - first

        @pl.when(jnp.logical_and(place >= 0, place < n // rows))
        def _(b=b, place=place):
            at = (pl.ds(b * rows, rows), pl.ds(pl.multiple_of(place * rows, rows), rows))
            s = sim[at]
            eye = lax.broadcasted_iota(jnp.int32, s.shape, 0) == lax.broadcasted_iota(jnp.int32, s.shape, 1)
            z = scale * s + bias
            w = -scale / (1.0 + jnp.exp(z))
            wgt[at] = jnp.where(eye, w, wgt[at].astype(F32)).astype(BF)
            z = jnp.where(eye, z, 0.0)
            sd = jnp.where(eye, s, 0.0)
            one = jnp.where(eye, 1.0, 0.0)
            for row, v in ((0, z), (8, one), (16, sd)):
                total = v[0:8]
                for k in range(1, rows // 8):
                    total = total + v[8 * k : 8 * k + 8]
                sums[row : row + 8, 0:rows] -= total


def scores_kernel(first, scal, diag, xa, xb, ta, tb, *refs):
    before = refs[:1] if len(refs) == 9 else ()
    wgt, out_sums, xs, ts, sim, sums, xsem, tsem = refs[-8:]
    rows = xa.shape[0] // 4
    x, t = Pending(block_copies((xa, xb), xs, xsem), rows), Pending(block_copies((ta, tb), ts, tsem), rows)
    for n in range(8):
        t.copies[n].start()
        x.copies[n].start()

    def need(r, c):
        x.upto(r)
        t.upto(c)

    scores(scal, diag, first, xs, ts, sim, wgt, sums, need)
    if before:
        total = sums[...] + before[0][...]
        lane = lax.broadcasted_iota(jnp.int32, (8, 128), 1)
        out = jnp.zeros((8, 128), F32)
        for k in range(3):
            out = jnp.where(lane == k, jnp.sum(total[8 * k : 8 * k + 8], keepdims=True), out)
        out_sums[...] = out[0:1]
    else:
        out_sums[...] = sums[...]


def score_half(first, scal, diag, images, texts, before=()):
    rows, d = images[0].shape[0] // 4, images[0].shape[1]
    m = n = 8 * rows
    return pl.pallas_call(
        lambda *refs: scores_kernel(first, *refs),
        in_specs=[SM, SM] + [ANY] * 4 + [VM] * len(before),
        out_specs=[VM, VM],
        out_shape=(sds((m, n), BF), sds((1, 128) if before else (24, PIECE), F32)),
        scratch_shapes=[
            pltpu.VMEM((m, d), BF),
            pltpu.VMEM((n, d), BF),
            pltpu.VMEM((m, n), F32),
            pltpu.VMEM((24, PIECE), F32),
            pltpu.SemaphoreType.DMA((8,)),
            pltpu.SemaphoreType.DMA((8,)),
        ],
        compiler_params=params(),
        cost_estimate=pl.CostEstimate(
            flops=2 * m * n * d, bytes_accessed=(m + n) * d * 2, transcendentals=3 * m * n
        ),
        name="scores",
    )(scal, diag, *images, *texts, *before)


def far_kernel(dims, l0, l1, r0a, r0b, r1a, r1b, out, lhs, rhs, lsem, s0, s1):
    n = rhs.shape[0] // 2
    p0 = Pending(block_copies((r0a, r0b), rhs, s0), n // 8)
    p1 = Pending(block_copies((r1a, r1b), rhs, s1, n), n // 8)
    cut = (pl.ds(0, STRIP), slice(None)) if dims == 1 else (slice(None), pl.ds(0, STRIP))
    lc = [pltpu.make_async_copy(l.at[cut], lhs.at[k], lsem.at[k]) for k, l in enumerate((l0, l1))]
    lc[0].start()
    p0.start()
    lc[1].start()
    p1.start()
    lc[0].wait()
    p0.upto(n)
    part = dot(lhs[0], rhs[:n, :], ((dims,), (0,)))
    lc[1].wait()
    p1.upto(n)
    out[...] = encode(part + dot(lhs[1], rhs[n:, :], ((dims,), (0,))))


def far_pull(dims, w0, w1, rows0, rows1, name):
    d = rows0[0].shape[1]
    n = w0.shape[dims]
    return pl.pallas_call(
        lambda *refs: far_kernel(dims, *refs),
        in_specs=[ANY] * 6,
        out_specs=VM,
        out_shape=sds((STRIP, d), BF),
        scratch_shapes=[
            pltpu.VMEM((2, STRIP, n) if dims == 1 else (2, n, STRIP), BF),
            pltpu.VMEM((2 * n, d), BF),
            pltpu.SemaphoreType.DMA((2,)),
            pltpu.SemaphoreType.DMA((8,)),
            pltpu.SemaphoreType.DMA((8,)),
        ],
        compiler_params=params(),
        cost_estimate=pl.CostEstimate(
            flops=4 * STRIP * n * d, bytes_accessed=4 * n * d + 4 * STRIP * n, transcendentals=0
        ),
        name=name,
    )(w0, w1, *rows0, *rows1)


def near_kernel(dims, l0, l1, r0a, r0b, r1a, r1b, *refs):
    o1, o3, own, w0, w1, rhs, pull, lsem, s0, s1 = refs
    n = rhs.shape[0] // 2
    p0 = Pending(block_copies((r0a, r0b), rhs, s0), n // 8)
    p1 = Pending(block_copies((r1a, r1b), rhs, s1, n), n // 8)
    lc = [pltpu.make_async_copy(s, w, lsem.at[k]) for k, (s, w) in enumerate(((l0, w0), (l1, w1)))]
    lc[0].start()
    p0.start()
    lc[1].start()
    p1.start()
    groups = [slice(SLOT[k] * STRIP, (SLOT[k] + 1) * STRIP) for k in (1, 3, 0)]
    cut = (lambda w, at: w[at, :]) if dims == 1 else (lambda w, at: w[:, at])
    lc[0].wait()
    p0.upto(n)
    for k, at in enumerate(groups):
        pull[k] = dot(cut(w0, at), rhs[:n, :], ((dims,), (0,)))
    lc[1].wait()
    p1.upto(n)
    for k, at in enumerate(groups):
        total = pull[k] + dot(cut(w1, at), rhs[n:, :], ((dims,), (0,)))
        (o1, o3, own)[k][...] = encode(total) if k < 2 else total


def near_pulls(dims, w0, w1, rows0, rows1, name):
    m, d = w0.shape[0], rows0[0].shape[1]
    return pl.pallas_call(
        lambda *refs: near_kernel(dims, *refs),
        in_specs=[ANY] * 6,
        out_specs=[VM] * 3,
        out_shape=(sds((STRIP, d), BF), sds((STRIP, d), BF), sds((STRIP, d), F32)),
        scratch_shapes=[pltpu.VMEM((m, m), BF)] * 2
        + [pltpu.VMEM((2 * m, d), BF), pltpu.VMEM((3, STRIP, d), F32), pltpu.SemaphoreType.DMA((2,))]
        + [pltpu.SemaphoreType.DMA((8,))] * 2,
        compiler_params=params(),
        cost_estimate=pl.CostEstimate(
            flops=3 * m * m * d, bytes_accessed=4 * m * d + 4 * m * m, transcendentals=0
        ),
        name=name,
    )(w0, w1, *rows0, *rows1)


def partner_kernel(own, c1, c2, c3, out):
    out[...] = encode(own[...] + decode(c1[...]) + decode(c2[...]) + decode(c3[...]))


def fold_partner(own, *codes):
    rows, d = own.shape[0] // 2, own.shape[1]
    half = pl.BlockSpec((rows, d), lambda i: (1, 0))
    return pl.pallas_call(
        partner_kernel,
        grid=(1,),
        in_specs=[half] * 4,
        out_specs=pl.BlockSpec((rows, d), lambda i: (0, 0)),
        out_shape=sds((rows, d), BF),
        compiler_params=params(),
        name="fold_partner",
    )(own, *codes)


def own_kernel(own, c1, c2, c3, out):
    out[...] = own[...] + decode(c1[...]) + decode(c2[...]) + decode(c3[...])


def fold_own(own, *codes):
    rows, d = own.shape[0] // 2, own.shape[1]
    half = pl.BlockSpec((rows, d), lambda i: (0, 0))
    return pl.pallas_call(
        own_kernel,
        grid=(1,),
        in_specs=[half] * 4,
        out_specs=half,
        out_shape=sds((rows, d), F32),
        compiler_params=params(),
        name="fold_own",
    )(own, *codes)


def finish_kernel(x_ref, own, code_ref, out_ref):
    x = x_ref[...]
    norm = jnp.sqrt(jnp.sum(x * x, axis=1, keepdims=True) + 1e-06)
    hat = x / norm
    pull = own[...] + decode(code_ref[...])
    out_ref[...] = (pull - hat * jnp.sum(hat * pull, axis=1, keepdims=True)) / norm


def finish(x, own, code):
    return pl.pallas_call(
        finish_kernel, out_shape=sds(x.shape, F32), compiler_params=params(), name="finish"
    )(x, own, code)


def img_index(y, z, c):
    return (y % 4) * 4 + (z % 2) * 2 + c % 2


def perm_x(shift):
    return [(i, ((i // 2 + shift) % 4) * 2 + i % 2) for i in range(8)]


def perm_y(shift):
    return [(i, img_index(i // 4 + shift, i // 2, i)) for i in range(16)]


PERM_ZHI = [(i, i ^ 1) for i in range(8)]
PERM_ZLO = [(i, i ^ 2) for i in range(16)]
PERM_CORE = [(i, i ^ 1) for i in range(16)]
send = lax.ppermute


def after(x, *others):
    return lax.optimization_barrier((x, *others))[0]


def gather(low, axis, perm, perm_z):
    a1, a3 = send(low, axis, perm(1)), send(low, axis, perm(-1))
    z = send(low, axis, perm_z)
    a2 = send(a1, axis, perm(1))
    z1, z3 = send(z, axis, perm(1)), send(z, axis, perm(-1))
    z2 = send(z3, axis, perm(-1))
    return jnp.concatenate([low, a1, a3, a2], 0), jnp.concatenate([z, z1, z3, z2], 0)


def exchange_sum(v, axis, bit):
    size = {"img": 16, "txt": 8}[axis]
    return v + send(v, axis, [(i, i ^ bit) for i in range(size)])


def local(image_embed, text_embed, log_scale, logit_bias):
    rows, d = image_embed.shape
    image_low, text_low = normalize(image_embed, text_embed)
    images = gather(image_low, "txt", perm_x, PERM_ZHI)
    own = gather(text_low, "img", perm_y, PERM_ZLO)
    other = [send(t, "img", PERM_CORE) for t in own]
    partner = [send(x, "img", PERM_CORE) for x in images]

    i, t = lax.axis_index("img"), lax.axis_index("txt")
    b = jnp.arange(8, dtype=jnp.int32)
    slot = b // 2
    ring = jnp.where(slot == 0, 2, jnp.where(slot == 1, 1, jnp.where(slot == 2, 3, 0)))
    g = 8 * i + ((t // 2 - ring) % 4) * 2 + ((t % 2) ^ (b % 2))
    o = g % 16
    k = (i // 4 - o // 4) % 4
    slot = jnp.where(k == 2, 0, jnp.where(k == 1, 1, jnp.where(k == 3, 2, 3)))
    mine = 1 - ((i % 2) ^ (o % 2))
    place = mine * 8 + slot * 2 + (((i // 2) % 2) ^ ((o // 2) % 2))
    diag = jnp.where(g // 16 == t, place, -1).astype(jnp.int32)
    scale = jnp.exp(log_scale)
    scal = jnp.stack([scale, logit_bias, scale * LOG2E, logit_bias * LOG2E])

    w_oth, sums = score_half(0, scal, diag, images, other)
    w_rec = send(w_oth, "img", PERM_CORE)
    w_own, v = score_half(8, scal, diag, images, own, (sums,))

    u = exchange_sum(v, "img", 4)
    i2 = far_pull(1, w_own, w_oth, own, other, "far_image")
    u = after(u, i2)
    i2 = send(i2, "txt", perm_x(2))
    v = exchange_sum(u, "img", 8)
    t2 = far_pull(0, after(w_own, u), w_rec, images, partner, "far_text")
    v = after(v, t2)
    t2 = send(t2, "img", perm_y(2))
    u = exchange_sum(v, "img", 2)
    i1, i3, i0 = near_pulls(1, after(w_own, v), w_oth, own, other, "near_image")
    u = after(u, i0)
    i1, i3 = after(i1, i2), after(i3, i2)
    i1, i3 = send(i1, "txt", perm_x(-1)), send(i3, "txt", perm_x(1))
    v = exchange_sum(u, "txt", 1)
    t1, t3, t0 = near_pulls(0, after(w_own, u), w_rec, images, partner, "near_text")
    v = after(v, t0)
    t1, t3 = after(t1, t2), after(t3, t2)
    t1, t3 = send(t1, "img", perm_y(-1)), send(t3, "img", perm_y(1))
    v = exchange_sum(v, "img", 1)
    v = after(v, i1, i3)
    v = exchange_sum(exchange_sum(v, "txt", 2), "txt", 4)
    t0 = after(t0, v)

    icodes, tcodes = (i1, i2, i3), (t1, t2, t3)
    image_code = send(fold_partner(i0, *icodes), "txt", PERM_ZHI)
    text_code = send(fold_partner(t0, *tcodes), "img", PERM_ZLO)
    image_grad = finish(image_embed, fold_own(i0, *icodes), image_code)
    text_grad = finish(text_embed, fold_own(t0, *tcodes), text_code)
    pairs = F32(128.0 * rows) * F32(128.0 * rows)
    return (v[0, 0] / pairs, image_grad, text_grad, v[0, 2] * scale / pairs, v[0, 1] / pairs)


def solution(mesh):
    placed = (P(("img", "txt"), None), P(("txt", "img"), None), P(), P())
    return jax.shard_map(
        local,
        mesh=mesh,
        in_specs=placed,
        out_specs=(P(), P(("img", "txt"), None), P(("txt", "img"), None), P(), P()),
        check_vma=False,
    )
```

```python
import jax
import jax.numpy as jnp
from jax import lax
from jax.experimental import pallas as pl
from jax.experimental.pallas import tpu as pltpu
from jax.sharding import PartitionSpec as P

BF = jnp.bfloat16
F32 = jnp.float32
LOG2E = 1.4426950408889634
VM = pl.BlockSpec(memory_space=pltpu.VMEM)
SM = pl.BlockSpec(memory_space=pltpu.SMEM)
PIECE = 512


def sds(shape, dtype):
    return jax.ShapeDtypeStruct(shape, dtype)


def params():
    return pltpu.CompilerParams(vmem_limit_bytes=24 * 1024 * 1024)


def small():
    return pltpu.CompilerParams(vmem_limit_bytes=8 * 1024 * 1024)


def encode(x):
    sq = x * x
    return (sq * sq * sq * x).astype(BF)


def decode(code):
    y = code.astype(F32)
    return y * jnp.exp2(jnp.log2(jnp.maximum(jnp.abs(y), 1.2e-38)) * (-6.0 / 7.0))


def dot(a, b, dims):
    return lax.dot_general(a, b, (dims, ((), ())), preferred_element_type=F32)


def normalize_kernel(a_ref, b_ref, a_out, b_out):
    for src, dst in ((a_ref, a_out), (b_ref, b_out)):
        x = src[...]
        norm = jnp.sqrt(jnp.sum(x * x, axis=1, keepdims=True) + 1e-06)
        dst[...] = (x / norm).astype(BF)


def normalize(a, b):
    return pl.pallas_call(
        normalize_kernel, out_shape=(sds(a.shape, BF), sds(b.shape, BF)), out_specs=[VM, VM], name="normalize"
    )(a, b)


RING = (0, 1, 3, 2)


def scores(scal, diag, first, xs, ts, sim, wgt, sums):
    tall, n, rows = xs[0].shape[0], 2 * ts[0].shape[0], xs[0].shape[0] // 4
    scale, bias, mult, shift = scal[0], scal[1], scal[2], scal[3]
    pieces = [(r, c) for r in range(2) for c in range(2)]

    def score(r, c):
        sim[r * tall : (r + 1) * tall, c * PIECE : (c + 1) * PIECE] = dot(xs[r][...], ts[c][...], ((1,), (1,)))

    acc = [jnp.zeros((8, PIECE), F32) for _ in range(3)]
    score(*pieces[0])
    for p, (r, c) in enumerate(pieces):
        if p + 1 < len(pieces):
            score(*pieces[p + 1])
        prod = None
        r, c = r * tall, c * PIECE
        for i in range(0, tall, 16):
            s = sim[r + i : r + i + 16, c : c + PIECE]
            e = jnp.exp2(s * mult + shift)
            u = e + 1.0
            r0 = pl.reciprocal(u, approx=True)
            sig = e * (r0 * (2.0 - u * r0))
            wgt[r + i : r + i + 16, c : c + PIECE] = (sig * scale).astype(BF)
            both = u[0:8] * u[8:16]
            prod = both if prod is None else prod * both
            if i % 64 == 48:
                acc[0] = acc[0] + jnp.log(prod)
                prod = None
            ss = sig * s
            acc[1] = acc[1] + (sig[0:8] + sig[8:16])
            acc[2] = acc[2] + (ss[0:8] + ss[8:16])
    for k in range(3):
        sums[8 * k : 8 * k + 8] = acc[k]

    for b in range(8):
        place = diag[b] - first

        @pl.when(jnp.logical_and(place >= 0, place < n // rows))
        def _(b=b, place=place):
            at = (pl.ds(b * rows, rows), pl.ds(pl.multiple_of(place * rows, rows), rows))
            s = sim[at]
            eye = lax.broadcasted_iota(jnp.int32, s.shape, 0) == lax.broadcasted_iota(jnp.int32, s.shape, 1)
            z = scale * s + bias
            w = -scale / (1.0 + jnp.exp(z))
            wgt[at] = jnp.where(eye, w, wgt[at].astype(F32)).astype(BF)
            z = jnp.where(eye, z, 0.0)
            sd = jnp.where(eye, s, 0.0)
            one = jnp.where(eye, 1.0, 0.0)
            for row, v in ((0, z), (8, one), (16, sd)):
                total = v[0:8]
                for k in range(1, rows // 8):
                    total = total + v[8 * k : 8 * k + 8]
                sums[row : row + 8, 0:rows] -= total


def here(*arrays):
    return [pltpu.with_memory_space_constraint(a, pltpu.VMEM) for a in arrays]


def scores_kernel(first, scal, diag, xa, xb, ta, tb, *refs):
    before = refs[:1] if len(refs) == 5 else ()
    wgt, out_sums, sim, sums = refs[-4:]
    scores(scal, diag, first, (xa, xb), (ta, tb), sim, wgt, sums)
    if before:
        total = sums[...] + before[0][...]
        lane = lax.broadcasted_iota(jnp.int32, (8, 128), 1)
        out = jnp.zeros((8, 128), F32)
        for k in range(3):
            out = jnp.where(lane == k, jnp.sum(total[8 * k : 8 * k + 8], keepdims=True), out)
        out_sums[...] = out[0:1]
    else:
        out_sums[...] = sums[...]


def score_half(first, scal, diag, images, texts, before=()):
    d = images[0].shape[1]
    m = n = 2 * images[0].shape[0]
    return pl.pallas_call(
        lambda *refs: scores_kernel(first, *refs),
        in_specs=[SM, SM] + [VM] * (4 + len(before)),
        out_specs=[VM, VM],
        out_shape=(sds((m, n), BF), sds((1, 128) if before else (24, PIECE), F32)),
        scratch_shapes=[pltpu.VMEM((m, n), F32), pltpu.VMEM((24, PIECE), F32)],
        compiler_params=params(),
        cost_estimate=pl.CostEstimate(
            flops=2 * m * n * d, bytes_accessed=(m + n) * d * 2, transcendentals=3 * m * n
        ),
        name="scores",
    )(scal, diag, *here(*images, *texts, *before))


def group_pull(dims, j, weights, pairs):
    total = None
    for w, pair in zip(weights, pairs):
        tall = pair[0].shape[0]
        rows = tall // 4
        one, two = slice(j * rows, (j + 1) * rows), slice(tall + j * rows, tall + (j + 1) * rows)
        for h, r in enumerate(pair):
            at = slice(h * tall, (h + 1) * tall)
            if dims == 1:
                lhs = jnp.concatenate([w[one, at], w[two, at]], 0)
            else:
                lhs = jnp.concatenate([w[at, one], w[at, two]], 1)
            part = dot(lhs, r[...], ((dims,), (0,)))
            total = part if total is None else total + part
    return total


def pulls_kernel(dims, groups, w0, w1, r0a, r0b, r1a, r1b, *outs):
    for j, out in zip(groups, outs):
        total = group_pull(dims, j, (w0, w1), ((r0a, r0b), (r1a, r1b)))
        out[...] = encode(total) if j else total


def pulls(dims, groups, w0, w1, rows0, rows1, name):
    rows, d = rows0[0].shape[0] // 4, rows0[0].shape[1]
    n = w0.shape[dims]
    out = pl.pallas_call(
        lambda *refs: pulls_kernel(dims, groups, *refs),
        in_specs=[VM] * 6,
        out_specs=[VM] * len(groups),
        out_shape=[sds((2 * rows, d), BF if j else F32) for j in groups],
        compiler_params=params(),
        cost_estimate=pl.CostEstimate(
            flops=8 * len(groups) * rows * n * d, bytes_accessed=4 * n * d, transcendentals=0
        ),
        name=name,
    )(*here(w0, w1, *rows0, *rows1))
    return out[0] if len(groups) == 1 else out


def partner_kernel(own, c1, c2, c3, out):
    at = pl.ds(out.shape[0], out.shape[0])
    out[...] = encode(own[at, :] + decode(c1[at, :]) + decode(c2[at, :]) + decode(c3[at, :]))


def fold_partner(own, *codes):
    rows, d = own.shape[0] // 2, own.shape[1]
    return pl.pallas_call(
        partner_kernel,
        in_specs=[VM] * 4,
        out_specs=VM,
        out_shape=sds((rows, d), BF),
        compiler_params=small(),
        name="fold_partner",
    )(*here(own, *codes))


def own_kernel(own, c1, c2, c3, out):
    at = pl.ds(0, out.shape[0])
    out[...] = own[at, :] + decode(c1[at, :]) + decode(c2[at, :]) + decode(c3[at, :])


def fold_own(own, *codes):
    rows, d = own.shape[0] // 2, own.shape[1]
    return pl.pallas_call(
        own_kernel,
        in_specs=[VM] * 4,
        out_specs=VM,
        out_shape=sds((rows, d), F32),
        compiler_params=small(),
        name="fold_own",
    )(*here(own, *codes))


def finish_kernel(x_ref, own, code_ref, out_ref):
    x = x_ref[...]
    norm = jnp.sqrt(jnp.sum(x * x, axis=1, keepdims=True) + 1e-06)
    hat = x / norm
    pull = own[...] + decode(code_ref[...])
    out_ref[...] = (pull - hat * jnp.sum(hat * pull, axis=1, keepdims=True)) / norm


def finish(x, own, code):
    return pl.pallas_call(
        finish_kernel,
        in_specs=[VM] * 3,
        out_specs=VM,
        out_shape=sds(x.shape, F32),
        compiler_params=small(),
        name="finish",
    )(x, *here(own, code))


def img_index(y, z, c):
    return (y % 4) * 4 + (z % 2) * 2 + c % 2


def perm_x(shift):
    return [(i, ((i // 2 + shift) % 4) * 2 + i % 2) for i in range(8)]


def perm_y(shift):
    return [(i, img_index(i // 4 + shift, i // 2, i)) for i in range(16)]


PERM_ZHI = [(i, i ^ 1) for i in range(8)]
PERM_ZLO = [(i, i ^ 2) for i in range(16)]
PERM_CORE = [(i, i ^ 1) for i in range(16)]
send = lax.ppermute


def after(x, *others):
    return lax.optimization_barrier((x, *others))[0]


def gather(low, axis, perm, perm_z):
    a1, a3 = send(low, axis, perm(1)), send(low, axis, perm(-1))
    z = send(low, axis, perm_z)
    a2 = send(a1, axis, perm(1))
    z1, z3 = send(z, axis, perm(1)), send(z, axis, perm(-1))
    z2 = send(z3, axis, perm(-1))
    return jnp.concatenate([low, a1, a3, a2], 0), jnp.concatenate([z, z1, z3, z2], 0)


def exchange_sum(v, axis, bit):
    size = {"img": 16, "txt": 8}[axis]
    return v + send(v, axis, [(i, i ^ bit) for i in range(size)])


def local(image_embed, text_embed, log_scale, logit_bias):
    rows, d = image_embed.shape
    image_low, text_low = normalize(image_embed, text_embed)
    images = gather(image_low, "txt", perm_x, PERM_ZHI)
    own = gather(text_low, "img", perm_y, PERM_ZLO)
    other = [send(t, "img", PERM_CORE) for t in own]
    partner = [send(x, "img", PERM_CORE) for x in images]

    i, t = lax.axis_index("img"), lax.axis_index("txt")
    b = jnp.arange(8, dtype=jnp.int32)
    j, zz = b % 4, b // 4
    ring = jnp.where(j == 2, 3, jnp.where(j == 3, 2, j))
    g = 8 * i + ((t // 2 - ring) % 4) * 2 + ((t % 2) ^ zz)
    o = g % 16
    k = (i // 4 - o // 4) % 4
    mine = 1 - ((i % 2) ^ (o % 2))
    place = mine * 8 + (((i // 2) % 2) ^ ((o // 2) % 2)) * 4 + jnp.where(k == 2, 3, jnp.where(k == 3, 2, k))
    diag = jnp.where(g // 16 == t, place, -1).astype(jnp.int32)
    scale = jnp.exp(log_scale)
    scal = jnp.stack([scale, logit_bias, scale * LOG2E, logit_bias * LOG2E])

    w_oth, sums = score_half(0, scal, diag, images, other)
    w_rec = send(w_oth, "img", PERM_CORE)
    w_own, v = score_half(8, scal, diag, images, own, (sums,))

    u = exchange_sum(v, "img", 4)
    i2 = pulls(1, (3,), w_own, w_oth, own, other, "far_image")
    u = after(u, i2)
    i2 = send(i2, "txt", perm_x(2))
    v = exchange_sum(u, "img", 8)
    t2 = pulls(0, (3,), after(w_own, u), w_rec, images, partner, "far_text")
    v = after(v, t2)
    t2 = send(t2, "img", perm_y(2))
    u = exchange_sum(v, "img", 2)
    i1, i3, i0 = pulls(1, (1, 2, 0), after(w_own, v), w_oth, own, other, "near_image")
    u = after(u, i0)
    i1, i3 = after(i1, i2), after(i3, i2)
    i1, i3 = send(i1, "txt", perm_x(-1)), send(i3, "txt", perm_x(1))
    v = exchange_sum(u, "txt", 1)
    t1, t3, t0 = pulls(0, (1, 2, 0), after(w_own, u), w_rec, images, partner, "near_text")
    v = after(v, t0)
    t1, t3 = after(t1, t2), after(t3, t2)
    t1, t3 = send(t1, "img", perm_y(-1)), send(t3, "img", perm_y(1))
    v = exchange_sum(v, "img", 1)
    v = after(v, i1, i3)
    v = exchange_sum(exchange_sum(v, "txt", 2), "txt", 4)
    t0 = after(t0, v)

    icodes, tcodes = (i1, i2, i3), (t1, t2, t3)
    image_code = send(fold_partner(i0, *icodes), "txt", PERM_ZHI)
    text_code = send(fold_partner(t0, *tcodes), "img", PERM_ZLO)
    image_grad = finish(image_embed, fold_own(i0, *icodes), image_code)
    text_grad = finish(text_embed, fold_own(t0, *tcodes), text_code)
    pairs = F32(128.0 * rows) * F32(128.0 * rows)
    return (v[0, 0] / pairs, image_grad, text_grad, v[0, 2] * scale / pairs, v[0, 1] / pairs)


def solution(mesh):
    placed = (P(("img", "txt"), None), P(("txt", "img"), None), P(), P())
    return jax.shard_map(
        local,
        mesh=mesh,
        in_specs=placed,
        out_specs=(P(), P(("img", "txt"), None), P(("txt", "img"), None), P(), P()),
        check_vma=False,
    )
```

```python
import functools

import jax
import jax.numpy as jnp
from jax import lax
from jax.experimental import pallas as pl
from jax.experimental.pallas import tpu as pltpu
from jax.sharding import PartitionSpec as P

BF = jnp.bfloat16
F32 = jnp.float32
LOG2E = 1.4426950408889634
VM = pl.BlockSpec(memory_space=pltpu.VMEM)
SM = pl.BlockSpec(memory_space=pltpu.SMEM)
PIECE = 512


def sds(shape, dtype):
    return jax.ShapeDtypeStruct(shape, dtype)


def params():
    return pltpu.CompilerParams(vmem_limit_bytes=24 * 1024 * 1024)


def small():
    return pltpu.CompilerParams(vmem_limit_bytes=8 * 1024 * 1024)


def encode(x):
    sq = x * x
    return (sq * sq * sq * x).astype(BF)


def decode(code):
    y = code.astype(F32)
    return y * jnp.exp2(jnp.log2(jnp.maximum(jnp.abs(y), 1.2e-38)) * (-6.0 / 7.0))


def normalize_kernel(a_ref, b_ref, *outs):
    for src, low, hat_out, norm_out in ((a_ref, *outs[:3]), (b_ref, *outs[3:])):
        x = src[...]
        norm = jnp.sqrt(jnp.sum(x * x, axis=1, keepdims=True) + 1e-06)
        hat = x / norm
        low[...] = hat.astype(BF)
        hat_out[...] = hat
        norm_out[...] = norm


def normalize(a, b):
    one = lambda x: (sds(x.shape, BF), sds(x.shape, F32), sds((x.shape[0], 1), F32))
    out = pl.pallas_call(
        normalize_kernel, out_shape=one(a) + one(b), out_specs=[VM] * 6, name="normalize"
    )(a, b)
    return out[:3], out[3:]


def dot(a, b, dims):
    return lax.dot_general(a, b, (dims, ((), ())), preferred_element_type=F32)


RING = (0, 1, 3, 2, 0, 1, 3, 2)
PARTNER = (0, 0, 0, 0, 1, 1, 1, 1)
GROUP = {0: (0, 4), 1: (1, 5), 2: (3, 7), 3: (2, 6)}


def scores(scal, diag, first, xs, ts, sim, wgt, sums):
    tall, n, rows = xs[0].shape[0], 2 * ts[0].shape[0], xs[0].shape[0] // 4
    scale, bias, mult, shift = scal[0], scal[1], scal[2], scal[3]
    pieces = [(r, c) for r in range(2) for c in range(2)]

    def score(r, c):
        sim[r * tall : (r + 1) * tall, c * PIECE : (c + 1) * PIECE] = dot(xs[r][...], ts[c][...], ((1,), (1,)))

    acc = [jnp.zeros((8, PIECE), F32) for _ in range(3)]
    score(*pieces[0])
    for p, (r, c) in enumerate(pieces):
        if p + 1 < len(pieces):
            score(*pieces[p + 1])
        prod = None
        r, c = r * tall, c * PIECE
        for i in range(0, tall, 16):
            s = sim[r + i : r + i + 16, c : c + PIECE]
            e = jnp.exp2(s * mult + shift)
            u = e + 1.0
            r0 = pl.reciprocal(u, approx=True)
            sig = e * (r0 * (2.0 - u * r0))
            wgt[r + i : r + i + 16, c : c + PIECE] = (sig * scale).astype(BF)
            both = u[0:8] * u[8:16]
            prod = both if prod is None else prod * both
            if i % 64 == 48:
                acc[0] = acc[0] + jnp.log(prod)
                prod = None
            ss = sig * s
            acc[1] = acc[1] + (sig[0:8] + sig[8:16])
            acc[2] = acc[2] + (ss[0:8] + ss[8:16])
    for k in range(3):
        sums[8 * k : 8 * k + 8] = acc[k]

    for b in range(8):
        place = diag[b] - first

        @pl.when(jnp.logical_and(place >= 0, place < n // rows))
        def _(b=b, place=place):
            at = (pl.ds(b * rows, rows), pl.ds(pl.multiple_of(place * rows, rows), rows))
            s = sim[at]
            eye = lax.broadcasted_iota(jnp.int32, s.shape, 0) == lax.broadcasted_iota(jnp.int32, s.shape, 1)
            z = scale * s + bias
            w = -scale / (1.0 + jnp.exp(z))
            wgt[at] = jnp.where(eye, w, wgt[at].astype(F32)).astype(BF)
            z = jnp.where(eye, z, 0.0)
            sd = jnp.where(eye, s, 0.0)
            one = jnp.where(eye, 1.0, 0.0)
            for row, v in ((0, z), (8, one), (16, sd)):
                total = v[0:8]
                for k in range(1, rows // 8):
                    total = total + v[8 * k : 8 * k + 8]
                sums[row : row + 8, 0:rows] -= total


def here(*arrays):
    return [pltpu.with_memory_space_constraint(a, pltpu.VMEM) for a in arrays]


def scores_kernel(first, scal, diag, xa, xb, ta, tb, *refs):
    before = refs[:1] if len(refs) == 5 else ()
    wgt, out_sums, sim, sums = refs[-4:]
    scores(scal, diag, first, (xa, xb), (ta, tb), sim, wgt, sums)
    if before:
        total = sums[...] + before[0][...]
        lane = lax.broadcasted_iota(jnp.int32, (8, 128), 1)
        out = jnp.zeros((8, 128), F32)
        for k in range(3):
            out = jnp.where(lane == k, jnp.sum(total[8 * k : 8 * k + 8], keepdims=True), out)
        out_sums[...] = out[0:1]
    else:
        out_sums[...] = sums[...]


def score_half(first, scal, diag, images, texts, before=()):
    d = images[0].shape[1]
    m = n = 2 * images[0].shape[0]
    return pl.pallas_call(
        lambda *refs: scores_kernel(first, *refs),
        in_specs=[SM, SM] + [VM] * (4 + len(before)),
        out_specs=[VM, VM],
        out_shape=(sds((m, n), BF), sds((1, 128) if before else (24, PIECE), F32)),
        scratch_shapes=[pltpu.VMEM((m, n), F32), pltpu.VMEM((24, PIECE), F32)],
        compiler_params=params(),
        cost_estimate=pl.CostEstimate(
            flops=2 * m * n * d, bytes_accessed=(m + n) * d * 2, transcendentals=3 * m * n
        ),
        name="scores",
    )(scal, diag, *here(*images, *texts, *before))


def group_pull(dims, k, weights, pairs):
    total = None
    for w, pair in zip(weights, pairs):
        tall = pair[0].shape[0]
        rows = tall // 4
        one, two = (slice(b * rows, (b + 1) * rows) for b in GROUP[k])
        for h, r in enumerate(pair):
            at = slice(h * tall, (h + 1) * tall)
            if dims == 1:
                lhs = jnp.concatenate([w[one, at], w[two, at]], 0)
            else:
                lhs = jnp.concatenate([w[at, one], w[at, two]], 1)
            part = dot(lhs, r[...], ((dims,), (0,)))
            total = part if total is None else total + part
    return total


def far_kernel(dims, w0, w1, r0a, r0b, r1a, r1b, out_a, out_b):
    total = group_pull(dims, 2, (w0, w1), ((r0a, r0b), (r1a, r1b)))
    rows = out_a.shape[0]
    out_a[...] = encode(total[:rows])
    out_b[...] = encode(total[rows:])


def near_kernel(dims, w0, w1, r0a, r0b, r1a, r1b, via_a, via_b, o1, o3, own):
    rows = via_a.shape[0]
    for k, out in ((1, o1), (3, o3), (0, own)):
        total = group_pull(dims, k, (w0, w1), ((r0a, r0b), (r1a, r1b)))
        one, two = total[:rows], total[rows:]
        if k == 0:
            out[...] = total
            continue
        if k == 1:
            two = two + decode(via_b[...])
        else:
            one = one + decode(via_a[...])
        out[:rows, :] = encode(one)
        out[rows:, :] = encode(two)


def pulls(dims, w0, w1, rows0, rows1, name, via=()):
    rows, d = rows0[0].shape[0] // 4, rows0[0].shape[1]
    n = w0.shape[dims]
    shapes = [sds((2 * rows, d), BF)] * 2 + [sds((2 * rows, d), F32)] if via else [sds((rows, d), BF)] * 2
    return pl.pallas_call(
        functools.partial(near_kernel if via else far_kernel, dims),
        in_specs=[VM] * (6 + len(via)),
        out_specs=[VM] * len(shapes),
        out_shape=shapes,
        compiler_params=params(),
        cost_estimate=pl.CostEstimate(
            flops=8 * (3 if via else 1) * rows * n * d, bytes_accessed=4 * n * d, transcendentals=0
        ),
        name=name,
    )(*here(w0, w1, *rows0, *rows1, *via))


def partner_kernel(own, c1, c3, out):
    at = pl.ds(out.shape[0], out.shape[0])
    out[...] = encode(own[at, :] + decode(c1[at, :]) + decode(c3[at, :]))


def own_kernel(own, c1, c3, out):
    at = pl.ds(0, out.shape[0])
    out[...] = own[at, :] + decode(c1[at, :]) + decode(c3[at, :])


def fold(kernel, own, codes, dtype, name):
    rows, d = own.shape[0] // 2, own.shape[1]
    return pl.pallas_call(
        kernel,
        in_specs=[VM] * 3,
        out_specs=VM,
        out_shape=sds((rows, d), dtype),
        compiler_params=small(),
        name=name,
    )(*here(own, *codes))


def finish_kernel(hat_ref, norm_ref, own, code_ref, out_ref):
    hat = hat_ref[...]
    pull = own[...] + decode(code_ref[...])
    out_ref[...] = (pull - hat * jnp.sum(hat * pull, axis=1, keepdims=True)) / norm_ref[...]


def finish(hat, norm, own, code):
    return pl.pallas_call(
        finish_kernel,
        in_specs=[VM] * 4,
        out_specs=VM,
        out_shape=sds(hat.shape, F32),
        compiler_params=small(),
        name="finish",
    )(*here(hat, norm, own, code))


def img_index(y, z, c):
    return (y % 4) * 4 + (z % 2) * 2 + c % 2


def perm_x(shift):
    return [(i, ((i // 2 + shift) % 4) * 2 + i % 2) for i in range(8)]


def perm_y(shift):
    return [(i, img_index(i // 4 + shift, i // 2, i)) for i in range(16)]


PERM_ZHI = [(i, i ^ 1) for i in range(8)]
PERM_ZLO = [(i, i ^ 2) for i in range(16)]
PERM_CORE = [(i, i ^ 1) for i in range(16)]
send = lax.ppermute


def after(x, *others):
    return lax.optimization_barrier((x, *others))[0]


def gather(image, text):
    ways = ((image, "txt", perm_x, PERM_ZHI), (text, "img", perm_y, PERM_ZLO))
    z = [send(low, axis, pz) for low, axis, _, pz in ways]
    a1 = [send(low, axis, perm(1)) for low, axis, perm, _ in ways]
    a3 = [send(low, axis, perm(-1)) for low, axis, perm, _ in ways]
    a2 = [send(a, axis, perm(1)) for a, (_, axis, perm, _) in zip(a1, ways)]
    z, a1, a3, a2 = lax.optimization_barrier((z, a1, a3, a2))
    z3 = [send(b, axis, perm(-1)) for b, (_, axis, perm, _) in zip(z, ways)]
    z1 = [send(b, axis, perm(1)) for b, (_, axis, perm, _) in zip(z, ways)]
    z3, z1 = lax.optimization_barrier((z3, z1))
    z2 = lax.optimization_barrier([send(b, axis, perm(-1)) for b, (_, axis, perm, _) in zip(z3, ways)])
    return [
        (jnp.concatenate([w[0], a1[n], a3[n], a2[n]], 0), jnp.concatenate([z[n], z1[n], z3[n], z2[n]], 0))
        for n, w in enumerate(ways)
    ]


def exchange_sum(v, axis, *perms):
    got = [send(v, a, p) for a, p in zip(axis, perms)]
    return v + got[0] if len(got) == 1 else (v + got[1]) + (got[0] + got[2])


def local(image_embed, text_embed, log_scale, logit_bias):
    rows, d = image_embed.shape
    (image_low, image_hat, image_norm), (text_low, text_hat, text_norm) = normalize(image_embed, text_embed)
    images, own = gather(image_low, text_low)
    other = [send(t, "img", PERM_CORE) for t in own]
    partner = [send(x, "img", PERM_CORE) for x in images]

    i, t = lax.axis_index("img"), lax.axis_index("txt")
    ring, zz = jnp.array(RING, jnp.int32), jnp.array(PARTNER, jnp.int32)
    g = 8 * i + ((t // 2 - ring) % 4) * 2 + ((t % 2) ^ zz)
    o = g % 16
    k, z = (i // 4 - o // 4) % 4, ((i // 2) % 2) ^ ((o // 2) % 2)
    mine = 1 - ((i % 2) ^ (o % 2))
    found = jnp.logical_and(k[:, None] == ring[None, :], z[:, None] == zz[None, :])
    place = mine * 8 + jnp.sum(jnp.where(found, jnp.arange(8, dtype=jnp.int32)[None, :], 0), 1)
    diag = jnp.where(g // 16 == t, place, -1).astype(jnp.int32)
    scale = jnp.exp(log_scale)
    scal = jnp.stack([scale, logit_bias, scale * LOG2E, logit_bias * LOG2E])

    w_own, sums = score_half(8, scal, diag, images, own)
    w_oth, v = score_half(0, scal, diag, images, other, (sums,))
    w_rec = send(w_oth, "img", PERM_CORE)

    ia, ib = pulls(1, w_own, w_oth, own, other, "far_image")
    ia, ib = send(ia, "txt", perm_x(1)), send(ib, "txt", perm_x(-1))
    ta, tb = pulls(0, w_own, w_rec, images, partner, "far_text")
    v = after(v, ta)
    ta, tb = send(ta, "img", perm_y(1)), send(tb, "img", perm_y(-1))
    v = exchange_sum(v, ("img",), PERM_CORE)
    i1, i3, i0 = pulls(1, w_own, w_oth, own, other, "near_image", (ia, ib))
    v = after(v, i0)
    i1, i3 = send(i1, "txt", perm_x(-1)), send(i3, "txt", perm_x(1))
    both = [(n, n ^ 17) for n in range(128)]
    v = exchange_sum(v, ("img", ("img", "txt"), "txt"), PERM_ZLO, both, PERM_ZHI)
    t1, t3, t0 = pulls(0, after(w_own, i0), w_rec, images, partner, "near_text", (ta, tb))
    v = after(v, t0)
    t1, t3 = send(t1, "img", perm_y(-1)), send(t3, "img", perm_y(1))

    image_code = send(fold(partner_kernel, i0, (i1, i3), BF, "fold_partner"), "txt", PERM_ZHI)
    image_own = fold(own_kernel, i0, (i1, i3), F32, "fold_own")
    v = after(v, i1, i3)
    v = exchange_sum(v, ("txt",) * 3, perm_x(1), perm_x(2), perm_x(-1))
    text_code = fold(partner_kernel, t0, (t1, t3), BF, "fold_partner")
    v = after(v, text_code)
    text_code = send(text_code, "img", PERM_ZLO)
    text_own = fold(own_kernel, t0, (t1, t3), F32, "fold_own")
    v = exchange_sum(v, ("img",) * 3, perm_y(1), perm_y(2), perm_y(-1))
    image_grad = finish(image_hat, image_norm, image_own, image_code)
    text_grad = finish(text_hat, text_norm, after(text_own, v), text_code)
    pairs = F32(128.0 * rows) * F32(128.0 * rows)
    return (v[0, 0] / pairs, image_grad, text_grad, v[0, 2] * scale / pairs, v[0, 1] / pairs)


def solution(mesh):
    placed = (P(("img", "txt"), None), P(("txt", "img"), None), P(), P())
    return jax.shard_map(
        local,
        mesh=mesh,
        in_specs=placed,
        out_specs=(P(), P(("img", "txt"), None), P(("txt", "img"), None), P(), P()),
        check_vma=False,
    )
```

```python
import functools

import jax
import jax.numpy as jnp
from jax import lax
from jax.experimental import pallas as pl
from jax.experimental.pallas import tpu as pltpu
from jax.sharding import PartitionSpec as P

BF = jnp.bfloat16
F32 = jnp.float32
LOG2E = 1.4426950408889634
VM = pl.BlockSpec(memory_space=pltpu.VMEM)
SM = pl.BlockSpec(memory_space=pltpu.SMEM)
PIECE = 512


def sds(shape, dtype):
    return jax.ShapeDtypeStruct(shape, dtype)


def params():
    return pltpu.CompilerParams(vmem_limit_bytes=24 * 1024 * 1024)


def small():
    return pltpu.CompilerParams(vmem_limit_bytes=8 * 1024 * 1024)


def encode(x):
    sq = x * x
    return (sq * sq * sq * x).astype(BF)


def decode(code):
    y = code.astype(F32)
    return y * jnp.exp2(jnp.log2(jnp.maximum(jnp.abs(y), 1.2e-38)) * (-6.0 / 7.0))


def normalize_kernel(a_ref, b_ref, *outs):
    for src, low, hat_out, norm_out in ((a_ref, *outs[:3]), (b_ref, *outs[3:])):
        x = src[...]
        norm = jnp.sqrt(jnp.sum(x * x, axis=1, keepdims=True) + 1e-06)
        hat = x / norm
        low[...] = hat.astype(BF)
        hat_out[...] = hat
        norm_out[...] = norm


def normalize(a, b):
    one = lambda x: (sds(x.shape, BF), sds(x.shape, F32), sds((x.shape[0], 1), F32))
    out = pl.pallas_call(
        normalize_kernel, out_shape=one(a) + one(b), out_specs=[VM] * 6, name="normalize"
    )(a, b)
    return out[:3], out[3:]


def dot(a, b, dims):
    return lax.dot_general(a, b, (dims, ((), ())), preferred_element_type=F32)


RING = (0, 1, 3, 2, 0, 1, 3, 2)
PARTNER = (0, 0, 0, 0, 1, 1, 1, 1)
GROUP = {0: (0, 4), 1: (1, 5), 2: (3, 7), 3: (2, 6)}


def scores(scal, diag, first, xs, ts, sim, wgt, sums):
    tall, n, rows = xs[0].shape[0], 2 * ts[0].shape[0], xs[0].shape[0] // 4
    scale, bias, mult, shift = scal[0], scal[1], scal[2], scal[3]
    pieces = [(r, c) for r in range(2) for c in range(2)]

    def score(r, c):
        sim[r * tall : (r + 1) * tall, c * PIECE : (c + 1) * PIECE] = dot(xs[r][...], ts[c][...], ((1,), (1,)))

    acc = [jnp.zeros((8, PIECE), F32) for _ in range(3)]
    score(*pieces[0])
    for p, (r, c) in enumerate(pieces):
        if p + 1 < len(pieces):
            score(*pieces[p + 1])
        prod = None
        r, c = r * tall, c * PIECE
        for i in range(0, tall, 16):
            s = sim[r + i : r + i + 16, c : c + PIECE]
            e = jnp.exp2(s * mult + shift)
            u = e + 1.0
            r0 = pl.reciprocal(u, approx=True)
            sig = e * (r0 * (2.0 - u * r0))
            wgt[r + i : r + i + 16, c : c + PIECE] = (sig * scale).astype(BF)
            both = u[0:8] * u[8:16]
            prod = both if prod is None else prod * both
            if i % 64 == 48:
                acc[0] = acc[0] + jnp.log(prod)
                prod = None
            ss = sig * s
            acc[1] = acc[1] + (sig[0:8] + sig[8:16])
            acc[2] = acc[2] + (ss[0:8] + ss[8:16])
    for k in range(3):
        sums[8 * k : 8 * k + 8] = acc[k]

    for b in range(8):
        place = diag[b] - first

        @pl.when(jnp.logical_and(place >= 0, place < n // rows))
        def _(b=b, place=place):
            at = (pl.ds(b * rows, rows), pl.ds(pl.multiple_of(place * rows, rows), rows))
            s = sim[at]
            eye = lax.broadcasted_iota(jnp.int32, s.shape, 0) == lax.broadcasted_iota(jnp.int32, s.shape, 1)
            z = scale * s + bias
            w = -scale / (1.0 + jnp.exp(z))
            wgt[at] = jnp.where(eye, w, wgt[at].astype(F32)).astype(BF)
            z = jnp.where(eye, z, 0.0)
            sd = jnp.where(eye, s, 0.0)
            one = jnp.where(eye, 1.0, 0.0)
            for row, v in ((0, z), (8, one), (16, sd)):
                total = v[0:8]
                for k in range(1, rows // 8):
                    total = total + v[8 * k : 8 * k + 8]
                sums[row : row + 8, 0:rows] -= total


def here(*arrays):
    return [pltpu.with_memory_space_constraint(a, pltpu.VMEM) for a in arrays]


def scores_kernel(first, scal, diag, xa, xb, ta, tb, *refs):
    before = refs[:1] if len(refs) == 5 else ()
    wgt, out_sums, sim, sums = refs[-4:]
    scores(scal, diag, first, (xa, xb), (ta, tb), sim, wgt, sums)
    if before:
        total = sums[...] + before[0][...]
        lane = lax.broadcasted_iota(jnp.int32, (8, 128), 1)
        out = jnp.zeros((8, 128), F32)
        for k in range(3):
            out = jnp.where(lane == k, jnp.sum(total[8 * k : 8 * k + 8], keepdims=True), out)
        out_sums[...] = out[0:1]
    else:
        out_sums[...] = sums[...]


def score_half(first, scal, diag, images, texts, before=()):
    d = images[0].shape[1]
    m = n = 2 * images[0].shape[0]
    return pl.pallas_call(
        lambda *refs: scores_kernel(first, *refs),
        in_specs=[SM, SM] + [VM] * (4 + len(before)),
        out_specs=[VM, VM],
        out_shape=(sds((m, n), BF), sds((1, 128) if before else (24, PIECE), F32)),
        scratch_shapes=[pltpu.VMEM((m, n), F32), pltpu.VMEM((24, PIECE), F32)],
        compiler_params=params(),
        cost_estimate=pl.CostEstimate(
            flops=2 * m * n * d, bytes_accessed=(m + n) * d * 2, transcendentals=3 * m * n
        ),
        name="scores",
    )(scal, diag, *here(*images, *texts, *before))


def group_pull(dims, k, weights, pairs):
    total = None
    for w, pair in zip(weights, pairs):
        tall = pair[0].shape[0]
        rows = tall // 4
        one, two = (slice(b * rows, (b + 1) * rows) for b in GROUP[k])
        for h, r in enumerate(pair):
            at = slice(h * tall, (h + 1) * tall)
            if dims == 1:
                lhs = jnp.concatenate([w[one, at], w[two, at]], 0)
            else:
                lhs = jnp.concatenate([w[at, one], w[at, two]], 1)
            part = dot(lhs, r[...], ((dims,), (0,)))
            total = part if total is None else total + part
    return total


def put_row(ref, at, row):
    zero = jnp.zeros((16, ref.shape[1] - 384), BF)
    for n in range(3):
        part = row.astype(BF)
        row = row - part.astype(F32)
        ref[at : at + 16, 128 * n : 128 * n + 128] = jnp.broadcast_to(part.astype(F32), (16, 128)).astype(BF)
    ref[at : at + 16, 384:] = zero


def get_row(ref, at):
    part = [ref[at : at + 16, 128 * n : 128 * n + 128].astype(F32)[0:1] for n in range(3)]
    return (part[0] + part[1]) + part[2]


def far_kernel(dims, w0, w1, r0a, r0b, r1a, r1b, *refs):
    out_a, out_b = refs[-2:]
    total = group_pull(dims, 2, (w0, w1), ((r0a, r0b), (r1a, r1b)))
    rows = total.shape[0] // 2
    for out, half in ((out_a, total[:rows]), (out_b, total[rows:])):
        out[:rows, :] = encode(half)
        if len(refs) == 3:
            put_row(out, rows, refs[0][...])


def near_kernel(dims, w0, w1, r0a, r0b, r1a, r1b, via_a, via_b, o1, o3, own, *sides):
    rows = own.shape[0] // 2
    for k, out in ((1, o1), (3, o3), (0, own)):
        total = group_pull(dims, k, (w0, w1), ((r0a, r0b), (r1a, r1b)))
        one, two = total[:rows], total[rows:]
        if k == 0:
            out[...] = total
            continue
        if k == 1:
            two = two + decode(via_b[:rows, :])
        else:
            one = one + decode(via_a[:rows, :])
        out[:rows, :] = encode(one)
        out[rows : 2 * rows, :] = encode(two)
    if sides:
        o1[2 * rows :, :] = via_b[rows:, :]
        sides[0][...] = get_row(via_a, rows) + get_row(via_b, rows)


def pulls(dims, w0, w1, rows0, rows1, name, via=(), row=()):
    rows, d = rows0[0].shape[0] // 4, rows0[0].shape[1]
    n = w0.shape[dims]
    if via:
        more = via[0].shape[0] - rows
        shapes = [sds((2 * rows + more, d), BF), sds((2 * rows, d), BF), sds((2 * rows, d), F32)]
        shapes += [sds((1, 128), F32)] if more else []
    else:
        shapes = [sds((rows + 16 * len(row), d), BF)] * 2
    return pl.pallas_call(
        functools.partial(near_kernel if via else far_kernel, dims),
        in_specs=[VM] * (6 + len(via) + len(row)),
        out_specs=[VM] * len(shapes),
        out_shape=shapes,
        compiler_params=params(),
        cost_estimate=pl.CostEstimate(
            flops=8 * (3 if via else 1) * rows * n * d, bytes_accessed=4 * n * d, transcendentals=0
        ),
        name=name,
    )(*here(w0, w1, *rows0, *rows1, *via, *row))


def image_partner_kernel(own, c1, c3, v, sides, out, v_out):
    partner_kernel(own, c1, c3, out)
    v_out[...] = (v[...] + get_row(c1, own.shape[0])) + sides[...]


def fold_image_partner(own, codes, v, sides):
    rows, d = own.shape[0] // 2, own.shape[1]
    return pl.pallas_call(
        image_partner_kernel,
        in_specs=[VM] * 5,
        out_specs=[VM] * 2,
        out_shape=(sds((rows, d), BF), sds((1, 128), F32)),
        compiler_params=small(),
        name="fold_image_partner",
    )(*here(own, *codes, v, sides))


def partner_kernel(own, c1, c3, out):
    at = pl.ds(out.shape[0], out.shape[0])
    out[...] = encode(own[at, :] + decode(c1[at, :]) + decode(c3[at, :]))


def own_kernel(own, c1, c3, out):
    at = pl.ds(0, out.shape[0])
    out[...] = own[at, :] + decode(c1[at, :]) + decode(c3[at, :])


def fold(kernel, own, codes, dtype, name):
    rows, d = own.shape[0] // 2, own.shape[1]
    return pl.pallas_call(
        kernel,
        in_specs=[VM] * 3,
        out_specs=VM,
        out_shape=sds((rows, d), dtype),
        compiler_params=small(),
        name=name,
    )(*here(own, *codes))


def finish_kernel(hat_ref, norm_ref, own, code_ref, out_ref):
    hat = hat_ref[...]
    pull = own[...] + decode(code_ref[...])
    out_ref[...] = (pull - hat * jnp.sum(hat * pull, axis=1, keepdims=True)) / norm_ref[...]


def finish(hat, norm, own, code):
    return pl.pallas_call(
        finish_kernel,
        in_specs=[VM] * 4,
        out_specs=VM,
        out_shape=sds(hat.shape, F32),
        compiler_params=small(),
        name="finish",
    )(*here(hat, norm, own, code))


def img_index(y, z, c):
    return (y % 4) * 4 + (z % 2) * 2 + c % 2


def perm_x(shift):
    return [(i, ((i // 2 + shift) % 4) * 2 + i % 2) for i in range(8)]


def perm_y(shift):
    return [(i, img_index(i // 4 + shift, i // 2, i)) for i in range(16)]


PERM_ZHI = [(i, i ^ 1) for i in range(8)]
PERM_ZLO = [(i, i ^ 2) for i in range(16)]
PERM_CORE = [(i, i ^ 1) for i in range(16)]
send = lax.ppermute


def after(x, *others):
    return lax.optimization_barrier((x, *others))[0]


def gather(image, text):
    ways = ((image, "txt", perm_x, PERM_ZHI), (text, "img", perm_y, PERM_ZLO))
    z = [send(low, axis, pz) for low, axis, _, pz in ways]
    a1 = [send(low, axis, perm(1)) for low, axis, perm, _ in ways]
    a3 = [send(low, axis, perm(-1)) for low, axis, perm, _ in ways]
    a2 = [send(a, axis, perm(1)) for a, (_, axis, perm, _) in zip(a1, ways)]
    z, a1, a3, a2 = lax.optimization_barrier((z, a1, a3, a2))
    z3 = [send(b, axis, perm(-1)) for b, (_, axis, perm, _) in zip(z, ways)]
    z1 = [send(b, axis, perm(1)) for b, (_, axis, perm, _) in zip(z, ways)]
    z3, z1 = lax.optimization_barrier((z3, z1))
    z2 = lax.optimization_barrier([send(b, axis, perm(-1)) for b, (_, axis, perm, _) in zip(z3, ways)])
    return [
        (jnp.concatenate([w[0], a1[n], a3[n], a2[n]], 0), jnp.concatenate([z[n], z1[n], z3[n], z2[n]], 0))
        for n, w in enumerate(ways)
    ]


def exchange_sum(v, axis, *perms):
    got = [send(v, a, p) for a, p in zip(axis, perms)]
    return v + got[0] if len(got) == 1 else (v + got[1]) + (got[0] + got[2])


def local(image_embed, text_embed, log_scale, logit_bias):
    rows, d = image_embed.shape
    (image_low, image_hat, image_norm), (text_low, text_hat, text_norm) = normalize(image_embed, text_embed)
    images, own = gather(image_low, text_low)
    other = [send(t, "img", PERM_CORE) for t in own]
    partner = [send(x, "img", PERM_CORE) for x in images]

    i, t = lax.axis_index("img"), lax.axis_index("txt")
    ring, zz = jnp.array(RING, jnp.int32), jnp.array(PARTNER, jnp.int32)
    g = 8 * i + ((t // 2 - ring) % 4) * 2 + ((t % 2) ^ zz)
    o = g % 16
    k, z = (i // 4 - o // 4) % 4, ((i // 2) % 2) ^ ((o // 2) % 2)
    mine = 1 - ((i % 2) ^ (o % 2))
    found = jnp.logical_and(k[:, None] == ring[None, :], z[:, None] == zz[None, :])
    place = mine * 8 + jnp.sum(jnp.where(found, jnp.arange(8, dtype=jnp.int32)[None, :], 0), 1)
    diag = jnp.where(g // 16 == t, place, -1).astype(jnp.int32)
    scale = jnp.exp(log_scale)
    scal = jnp.stack([scale, logit_bias, scale * LOG2E, logit_bias * LOG2E])

    w_own, sums = score_half(8, scal, diag, images, own)
    w_oth, v = score_half(0, scal, diag, images, other, (sums,))
    w_rec = send(w_oth, "img", PERM_CORE)

    ia, ib = pulls(1, w_own, w_oth, own, other, "far_image", row=(v,))
    ia, ib = send(ia, "txt", perm_x(1)), send(ib, "txt", perm_x(-1))
    ta, tb = pulls(0, w_own, w_rec, images, partner, "far_text")
    ta, tb = send(ta, "img", perm_y(1)), send(tb, "img", perm_y(-1))
    i1, i3, i0, sides = pulls(1, w_own, w_oth, own, other, "near_image", (ia, ib))
    i1, i3 = send(i1, "txt", perm_x(-1)), send(i3, "txt", perm_x(1))
    t1, t3, t0 = pulls(0, after(w_own, i0), w_rec, images, partner, "near_text", (ta, tb))
    t1, t3 = send(t1, "img", perm_y(-1)), send(t3, "img", perm_y(1))

    image_code, v = fold_image_partner(i0, (i1, i3), v, sides)
    image_code = send(image_code, "txt", PERM_ZHI)
    image_own = fold(own_kernel, i0, (i1, i3), F32, "fold_own")
    v = exchange_sum(v, ("img",), PERM_CORE)
    both = [(n, n ^ 17) for n in range(128)]
    v = exchange_sum(v, ("img", ("img", "txt"), "txt"), PERM_ZLO, both, PERM_ZHI)
    text_code = fold(partner_kernel, t0, (t1, t3), BF, "fold_partner")
    text_code = send(text_code, "img", PERM_ZLO)
    text_own = fold(own_kernel, t0, (t1, t3), F32, "fold_own")
    v = exchange_sum(v, ("img",) * 3, perm_y(1), perm_y(2), perm_y(-1))
    image_grad = finish(image_hat, image_norm, image_own, image_code)
    text_grad = finish(text_hat, text_norm, after(text_own, v), text_code)
    pairs = F32(128.0 * rows) * F32(128.0 * rows)
    return (v[0, 0] / pairs, image_grad, text_grad, v[0, 2] * scale / pairs, v[0, 1] / pairs)


def solution(mesh):
    placed = (P(("img", "txt"), None), P(("txt", "img"), None), P(), P())
    return jax.shard_map(
        local,
        mesh=mesh,
        in_specs=placed,
        out_specs=(P(), P(("img", "txt"), None), P(("txt", "img"), None), P(), P()),
        check_vma=False,
    )
```

```python
import functools

import jax
import jax.numpy as jnp
from jax import lax
from jax.experimental import pallas as pl
from jax.experimental.pallas import tpu as pltpu
from jax.sharding import PartitionSpec as P

BF = jnp.bfloat16
F32 = jnp.float32
LOG2E = 1.4426950408889634
VM = pl.BlockSpec(memory_space=pltpu.VMEM)
SM = pl.BlockSpec(memory_space=pltpu.SMEM)
PIECE = 512


def sds(shape, dtype):
    return jax.ShapeDtypeStruct(shape, dtype)


def params():
    return pltpu.CompilerParams(vmem_limit_bytes=24 * 1024 * 1024)


def small():
    return pltpu.CompilerParams(vmem_limit_bytes=8 * 1024 * 1024)


def encode(x):
    sq = x * x
    return (sq * sq * sq * x).astype(BF)


def decode(code):
    y = code.astype(F32)
    return y * jnp.exp2(jnp.log2(jnp.maximum(jnp.abs(y), 1.2e-38)) * (-6.0 / 7.0))


def normalize_kernel(a_ref, b_ref, *outs):
    for src, low, hat_out, norm_out in ((a_ref, *outs[:3]), (b_ref, *outs[3:])):
        x = src[...]
        norm = jnp.sqrt(jnp.sum(x * x, axis=1, keepdims=True) + 1e-06)
        hat = x / norm
        low[...] = hat.astype(BF)
        hat_out[...] = hat
        norm_out[...] = norm


def normalize(a, b):
    one = lambda x: (sds(x.shape, BF), sds(x.shape, F32), sds((x.shape[0], 1), F32))
    out = pl.pallas_call(
        normalize_kernel, out_shape=one(a) + one(b), out_specs=[VM] * 6, name="normalize"
    )(a, b)
    return out[:3], out[3:]


def dot(a, b, dims):
    return lax.dot_general(a, b, (dims, ((), ())), preferred_element_type=F32)


RING = (0, 1, 3, 2, 0, 1, 3, 2)
PARTNER = (0, 0, 0, 0, 1, 1, 1, 1)
GROUP = {0: (0, 4), 1: (1, 5), 2: (3, 7), 3: (2, 6)}


def scores(scal, diag, first, xs, ts, sim, wgt, sums):
    tall, n, rows = xs[0].shape[0], 2 * ts[0].shape[0], xs[0].shape[0] // 4
    scale, bias, mult, shift = scal[0], scal[1], scal[2], scal[3]
    pieces = [(r, c) for r in range(2) for c in range(2)]

    def score(r, c):
        sim[r * tall : (r + 1) * tall, c * PIECE : (c + 1) * PIECE] = dot(xs[r][...], ts[c][...], ((1,), (1,)))

    acc = [jnp.zeros((8, PIECE), F32) for _ in range(3)]
    score(*pieces[0])
    for p, (r, c) in enumerate(pieces):
        if p + 1 < len(pieces):
            score(*pieces[p + 1])
        prod = None
        r, c = r * tall, c * PIECE
        for i in range(0, tall, 16):
            s = sim[r + i : r + i + 16, c : c + PIECE]
            e = jnp.exp2(s * mult + shift)
            u = e + 1.0
            r0 = pl.reciprocal(u, approx=True)
            sig = e * (r0 * (2.0 - u * r0))
            wgt[r + i : r + i + 16, c : c + PIECE] = (sig * scale).astype(BF)
            both = u[0:8] * u[8:16]
            prod = both if prod is None else prod * both
            if i % 64 == 48:
                acc[0] = acc[0] + jnp.log(prod)
                prod = None
            ss = sig * s
            acc[1] = acc[1] + (sig[0:8] + sig[8:16])
            acc[2] = acc[2] + (ss[0:8] + ss[8:16])
    for k in range(3):
        sums[8 * k : 8 * k + 8] = acc[k]

    for b in range(8):
        place = diag[b] - first

        @pl.when(jnp.logical_and(place >= 0, place < n // rows))
        def _(b=b, place=place):
            at = (pl.ds(b * rows, rows), pl.ds(pl.multiple_of(place * rows, rows), rows))
            s = sim[at]
            eye = lax.broadcasted_iota(jnp.int32, s.shape, 0) == lax.broadcasted_iota(jnp.int32, s.shape, 1)
            z = scale * s + bias
            w = -scale / (1.0 + jnp.exp(z))
            wgt[at] = jnp.where(eye, w, wgt[at].astype(F32)).astype(BF)
            z = jnp.where(eye, z, 0.0)
            sd = jnp.where(eye, s, 0.0)
            one = jnp.where(eye, 1.0, 0.0)
            for row, v in ((0, z), (8, one), (16, sd)):
                total = v[0:8]
                for k in range(1, rows // 8):
                    total = total + v[8 * k : 8 * k + 8]
                sums[row : row + 8, 0:rows] -= total


def here(*arrays):
    return [pltpu.with_memory_space_constraint(a, pltpu.VMEM) for a in arrays]


def scores_kernel(first, scal, diag, xa, xb, ta, tb, *refs):
    before = refs[:1] if len(refs) == 5 else ()
    wgt, out_sums, sim, sums = refs[-4:]
    scores(scal, diag, first, (xa, xb), (ta, tb), sim, wgt, sums)
    if before:
        total = sums[...] + before[0][...]
        lane = lax.broadcasted_iota(jnp.int32, (8, 128), 1)
        out = jnp.zeros((8, 128), F32)
        for k in range(3):
            out = jnp.where(lane == k, jnp.sum(total[8 * k : 8 * k + 8], keepdims=True), out)
        out_sums[...] = out[0:1]
    else:
        out_sums[...] = sums[...]


def score_half(first, scal, diag, images, texts, before=()):
    d = images[0].shape[1]
    m = n = 2 * images[0].shape[0]
    return pl.pallas_call(
        lambda *refs: scores_kernel(first, *refs),
        in_specs=[SM, SM] + [VM] * (4 + len(before)),
        out_specs=[VM, VM],
        out_shape=(sds((m, n), BF), sds((1, 128) if before else (24, PIECE), F32)),
        scratch_shapes=[pltpu.VMEM((m, n), F32), pltpu.VMEM((24, PIECE), F32)],
        compiler_params=params(),
        cost_estimate=pl.CostEstimate(
            flops=2 * m * n * d, bytes_accessed=(m + n) * d * 2, transcendentals=3 * m * n
        ),
        name="scores",
    )(scal, diag, *here(*images, *texts, *before))


def group_pull(dims, k, weights, pairs):
    total = None
    for w, pair in zip(weights, pairs):
        tall = pair[0].shape[0]
        rows = tall // 4
        one, two = (slice(b * rows, (b + 1) * rows) for b in GROUP[k])
        for h, r in enumerate(pair):
            at = slice(h * tall, (h + 1) * tall)
            if dims == 1:
                lhs = jnp.concatenate([w[one, at], w[two, at]], 0)
            else:
                lhs = jnp.concatenate([w[at, one], w[at, two]], 1)
            part = dot(lhs, r[...], ((dims,), (0,)))
            total = part if total is None else total + part
    return total


def put_row(ref, at, row):
    zero = jnp.zeros((16, ref.shape[1] - 384), BF)
    for n in range(3):
        part = row.astype(BF)
        row = row - part.astype(F32)
        ref[at : at + 16, 128 * n : 128 * n + 128] = jnp.broadcast_to(part.astype(F32), (16, 128)).astype(BF)
    ref[at : at + 16, 384:] = zero


def get_row(ref, at):
    part = [ref[at : at + 16, 128 * n : 128 * n + 128].astype(F32)[0:1] for n in range(3)]
    return (part[0] + part[1]) + part[2]


def far_kernel(dims, w0, w1, r0a, r0b, r1a, r1b, *refs):
    out_a, out_b = refs[-2:]
    total = group_pull(dims, 2, (w0, w1), ((r0a, r0b), (r1a, r1b)))
    rows = total.shape[0] // 2
    for out, half in ((out_a, total[:rows]), (out_b, total[rows:])):
        out[:rows, :] = encode(half)
        if len(refs) == 3:
            put_row(out, rows, refs[0][...])


def near_kernel(dims, w0, w1, r0a, r0b, r1a, r1b, via_a, via_b, o1, o3, own, *sides):
    rows = own.shape[0] // 2
    for k, out in ((1, o1), (3, o3), (0, own)):
        total = group_pull(dims, k, (w0, w1), ((r0a, r0b), (r1a, r1b)))
        one, two = total[:rows], total[rows:]
        if k == 0:
            out[...] = total
            continue
        if k == 1:
            two = two + decode(via_b[:rows, :])
        else:
            one = one + decode(via_a[:rows, :])
        out[:rows, :] = encode(one)
        out[rows : 2 * rows, :] = encode(two)
    if sides:
        o1[2 * rows :, :] = via_b[rows:, :]
        sides[0][...] = get_row(via_a, rows) + get_row(via_b, rows)


def pulls(dims, w0, w1, rows0, rows1, name, via=(), row=()):
    rows, d = rows0[0].shape[0] // 4, rows0[0].shape[1]
    n = w0.shape[dims]
    if via:
        more = via[0].shape[0] - rows
        shapes = [sds((2 * rows + more, d), BF), sds((2 * rows, d), BF), sds((2 * rows, d), F32)]
        shapes += [sds((1, 128), F32)] if more else []
    else:
        shapes = [sds((rows + 16 * len(row), d), BF)] * 2
    return pl.pallas_call(
        functools.partial(near_kernel if via else far_kernel, dims),
        in_specs=[VM] * (6 + len(via) + len(row)),
        out_specs=[VM] * len(shapes),
        out_shape=shapes,
        compiler_params=params(),
        cost_estimate=pl.CostEstimate(
            flops=8 * (3 if via else 1) * rows * n * d, bytes_accessed=4 * n * d, transcendentals=0
        ),
        name=name,
    )(*here(w0, w1, *rows0, *rows1, *via, *row))


def image_partner_kernel(own, c1, c3, v, sides, out, v_out):
    partner_kernel(own, c1, c3, out)
    v_out[...] = (v[...] + get_row(c1, own.shape[0])) + sides[...]


def fold_image_partner(own, codes, v, sides):
    rows, d = own.shape[0] // 2, own.shape[1]
    return pl.pallas_call(
        image_partner_kernel,
        in_specs=[VM] * 5,
        out_specs=[VM] * 2,
        out_shape=(sds((rows, d), BF), sds((1, 128), F32)),
        compiler_params=small(),
        name="fold_image_partner",
    )(*here(own, *codes, v, sides))


def partner_kernel(own, c1, c3, out):
    at = pl.ds(out.shape[0], out.shape[0])
    out[...] = encode(own[at, :] + decode(c1[at, :]) + decode(c3[at, :]))


def own_kernel(own, c1, c3, out):
    at = pl.ds(0, out.shape[0])
    out[...] = own[at, :] + decode(c1[at, :]) + decode(c3[at, :])


def fold(kernel, own, codes, dtype, name):
    rows, d = own.shape[0] // 2, own.shape[1]
    return pl.pallas_call(
        kernel,
        in_specs=[VM] * 3,
        out_specs=VM,
        out_shape=sds((rows, d), dtype),
        compiler_params=small(),
        name=name,
    )(*here(own, *codes))


def finish_kernel(hat_ref, norm_ref, own, code_ref, out_ref):
    hat = hat_ref[...]
    pull = own[...] + decode(code_ref[...])
    out_ref[...] = (pull - hat * jnp.sum(hat * pull, axis=1, keepdims=True)) / norm_ref[...]


def finish(hat, norm, own, code):
    return pl.pallas_call(
        finish_kernel,
        in_specs=[VM] * 4,
        out_specs=VM,
        out_shape=sds(hat.shape, F32),
        compiler_params=small(),
        name="finish",
    )(*here(hat, norm, own, code))


def img_index(y, z, c):
    return (y % 4) * 4 + (z % 2) * 2 + c % 2


def perm_x(shift):
    return [(i, ((i // 2 + shift) % 4) * 2 + i % 2) for i in range(8)]


def perm_y(shift):
    return [(i, img_index(i // 4 + shift, i // 2, i)) for i in range(16)]


PERM_ZHI = [(i, i ^ 1) for i in range(8)]
PERM_ZLO = [(i, i ^ 2) for i in range(16)]
PERM_CORE = [(i, i ^ 1) for i in range(16)]
send = lax.ppermute


def after(x, *others):
    return lax.optimization_barrier((x, *others))[0]


def gather(image, text):
    ways = ((image, "txt", perm_x, PERM_ZHI), (text, "img", perm_y, PERM_ZLO))
    z = [send(low, axis, pz) for low, axis, _, pz in ways]
    a1 = [send(low, axis, perm(1)) for low, axis, perm, _ in ways]
    a3 = [send(low, axis, perm(-1)) for low, axis, perm, _ in ways]
    a2 = [send(a, axis, perm(1)) for a, (_, axis, perm, _) in zip(a1, ways)]
    z, a1, a3, a2 = lax.optimization_barrier((z, a1, a3, a2))
    z3 = [send(b, axis, perm(-1)) for b, (_, axis, perm, _) in zip(z, ways)]
    z1 = [send(b, axis, perm(1)) for b, (_, axis, perm, _) in zip(z, ways)]
    z3, z1 = lax.optimization_barrier((z3, z1))
    z2 = lax.optimization_barrier([send(b, axis, perm(-1)) for b, (_, axis, perm, _) in zip(z3, ways)])
    return [
        (jnp.concatenate([w[0], a1[n], a3[n], a2[n]], 0), jnp.concatenate([z[n], z1[n], z3[n], z2[n]], 0))
        for n, w in enumerate(ways)
    ]


def exchange_sum(v, axis, *perms):
    got = [send(v, a, p) for a, p in zip(axis, perms)]
    return v + got[0] if len(got) == 1 else (v + got[1]) + (got[0] + got[2])


def local(image_embed, text_embed, log_scale, logit_bias):
    rows, d = image_embed.shape
    (image_low, image_hat, image_norm), (text_low, text_hat, text_norm) = normalize(image_embed, text_embed)
    images, own = gather(image_low, text_low)
    other = [send(t, "img", PERM_CORE) for t in own]
    partner = [send(x, "img", PERM_CORE) for x in images]

    i, t = lax.axis_index("img"), lax.axis_index("txt")
    ring, zz = jnp.array(RING, jnp.int32), jnp.array(PARTNER, jnp.int32)
    g = 8 * i + ((t // 2 - ring) % 4) * 2 + ((t % 2) ^ zz)
    o = g % 16
    k, z = (i // 4 - o // 4) % 4, ((i // 2) % 2) ^ ((o // 2) % 2)
    mine = 1 - ((i % 2) ^ (o % 2))
    found = jnp.logical_and(k[:, None] == ring[None, :], z[:, None] == zz[None, :])
    place = mine * 8 + jnp.sum(jnp.where(found, jnp.arange(8, dtype=jnp.int32)[None, :], 0), 1)
    diag = jnp.where(g // 16 == t, place, -1).astype(jnp.int32)
    scale = jnp.exp(log_scale)
    scal = jnp.stack([scale, logit_bias, scale * LOG2E, logit_bias * LOG2E])

    w_own, sums = score_half(8, scal, diag, images, own)
    w_oth, v = score_half(0, scal, diag, images, other, (sums,))
    w_rec = send(w_oth, "img", PERM_CORE)

    ia, ib = pulls(1, w_own, w_oth, own, other, "far_image", row=(v,))
    ia, ib = send(ia, "txt", perm_x(1)), send(ib, "txt", perm_x(-1))
    ta, tb = pulls(0, w_own, w_rec, images, partner, "far_text")
    ta, tb = send(ta, "img", perm_y(1)), send(tb, "img", perm_y(-1))
    i1, i3, i0, sides = pulls(1, w_own, w_oth, own, other, "near_image", (ia, ib))
    i1, i3 = send(i1, "txt", perm_x(-1)), send(i3, "txt", perm_x(1))
    t1, t3, t0 = pulls(0, after(w_own, i0), w_rec, images, partner, "near_text", (ta, tb))
    t1, t3 = send(t1, "img", perm_y(-1)), send(t3, "img", perm_y(1))

    image_code, v = fold_image_partner(i0, (i1, i3), v, sides)
    image_code = send(image_code, "txt", PERM_ZHI)
    image_own = fold(own_kernel, i0, (i1, i3), F32, "fold_own")
    v = exchange_sum(v, ("img",), PERM_CORE)
    both = [(n, n ^ 17) for n in range(128)]
    v = exchange_sum(v, ("img", ("img", "txt"), "txt"), PERM_ZLO, both, PERM_ZHI)
    text_code = fold(partner_kernel, t0, (t1, t3), BF, "fold_partner")
    v = after(v, text_code)
    text_code = send(text_code, "img", PERM_ZLO)
    text_own = fold(own_kernel, t0, (t1, t3), F32, "fold_own")
    v = exchange_sum(v, ("img",) * 3, perm_y(1), perm_y(2), perm_y(-1))
    image_grad = finish(image_hat, image_norm, image_own, image_code)
    text_grad = finish(text_hat, text_norm, after(text_own, v), text_code)
    pairs = F32(128.0 * rows) * F32(128.0 * rows)
    return (v[0, 0] / pairs, image_grad, text_grad, v[0, 2] * scale / pairs, v[0, 1] / pairs)


def solution(mesh):
    placed = (P(("img", "txt"), None), P(("txt", "img"), None), P(), P())
    return jax.shard_map(
        local,
        mesh=mesh,
        in_specs=placed,
        out_specs=(P(), P(("img", "txt"), None), P(("txt", "img"), None), P(), P()),
        check_vma=False,
    )
```

```python
import functools

import jax
import jax.numpy as jnp
from jax import lax
from jax.experimental import pallas as pl
from jax.experimental.pallas import tpu as pltpu
from jax.sharding import PartitionSpec as P

BF = jnp.bfloat16
F32 = jnp.float32
LOG2E = 1.4426950408889634
VM = pl.BlockSpec(memory_space=pltpu.VMEM)
SM = pl.BlockSpec(memory_space=pltpu.SMEM)
PIECE = 512


def sds(shape, dtype):
    return jax.ShapeDtypeStruct(shape, dtype)


def params():
    return pltpu.CompilerParams(vmem_limit_bytes=24 * 1024 * 1024)


def small():
    return pltpu.CompilerParams(vmem_limit_bytes=8 * 1024 * 1024)


def encode(x):
    sq = x * x
    return (sq * sq * sq * x).astype(BF)


def decode(code):
    y = code.astype(F32)
    return y * jnp.exp2(jnp.log2(jnp.maximum(jnp.abs(y), 1.2e-38)) * (-6.0 / 7.0))


def normalize_kernel(a_ref, b_ref, *outs):
    for src, low, hat_out, norm_out in ((a_ref, *outs[:3]), (b_ref, *outs[3:])):
        x = src[...]
        norm = jnp.sqrt(jnp.sum(x * x, axis=1, keepdims=True) + 1e-06)
        hat = x / norm
        low[...] = hat.astype(BF)
        hat_out[...] = hat
        norm_out[...] = norm


def normalize(a, b):
    one = lambda x: (sds(x.shape, BF), sds(x.shape, F32), sds((x.shape[0], 1), F32))
    out = pl.pallas_call(
        normalize_kernel, out_shape=one(a) + one(b), out_specs=[VM] * 6, name="normalize"
    )(a, b)
    return out[:3], out[3:]


def dot(a, b, dims):
    return lax.dot_general(a, b, (dims, ((), ())), preferred_element_type=F32)


RING = (0, 1, 3, 2, 0, 1, 3, 2)
PARTNER = (0, 0, 0, 0, 1, 1, 1, 1)
GROUP = {0: (0, 4), 1: (1, 5), 2: (3, 7), 3: (2, 6)}


def scores(scal, diag, first, xs, ts, sim, wgt, sums):
    tall, n, rows = xs[0].shape[0], 2 * ts[0].shape[0], xs[0].shape[0] // 4
    scale, bias, mult, shift = scal[0], scal[1], scal[2], scal[3]
    pieces = [(r, c) for r in range(2) for c in range(2)]

    def score(r, c):
        sim[r * tall : (r + 1) * tall, c * PIECE : (c + 1) * PIECE] = dot(xs[r][...], ts[c][...], ((1,), (1,)))

    acc = [jnp.zeros((8, PIECE), F32) for _ in range(3)]
    score(*pieces[0])
    for p, (r, c) in enumerate(pieces):
        if p + 1 < len(pieces):
            score(*pieces[p + 1])
        prod = None
        r, c = r * tall, c * PIECE
        for i in range(0, tall, 16):
            s = sim[r + i : r + i + 16, c : c + PIECE]
            e = jnp.exp2(s * mult + shift)
            u = e + 1.0
            r0 = pl.reciprocal(u, approx=True)
            sig = e * (r0 * (2.0 - u * r0))
            wgt[r + i : r + i + 16, c : c + PIECE] = (sig * scale).astype(BF)
            both = u[0:8] * u[8:16]
            prod = both if prod is None else prod * both
            if i % 64 == 48:
                acc[0] = acc[0] + jnp.log(prod)
                prod = None
            ss = sig * s
            acc[1] = acc[1] + (sig[0:8] + sig[8:16])
            acc[2] = acc[2] + (ss[0:8] + ss[8:16])
    for k in range(3):
        sums[8 * k : 8 * k + 8] = acc[k]

    for b in range(8):
        place = diag[b] - first

        @pl.when(jnp.logical_and(place >= 0, place < n // rows))
        def _(b=b, place=place):
            at = (pl.ds(b * rows, rows), pl.ds(pl.multiple_of(place * rows, rows), rows))
            s = sim[at]
            eye = lax.broadcasted_iota(jnp.int32, s.shape, 0) == lax.broadcasted_iota(jnp.int32, s.shape, 1)
            z = scale * s + bias
            w = -scale / (1.0 + jnp.exp(z))
            wgt[at] = jnp.where(eye, w, wgt[at].astype(F32)).astype(BF)
            z = jnp.where(eye, z, 0.0)
            sd = jnp.where(eye, s, 0.0)
            one = jnp.where(eye, 1.0, 0.0)
            for row, v in ((0, z), (8, one), (16, sd)):
                total = v[0:8]
                for k in range(1, rows // 8):
                    total = total + v[8 * k : 8 * k + 8]
                sums[row : row + 8, 0:rows] -= total


def here(*arrays):
    return [pltpu.with_memory_space_constraint(a, pltpu.VMEM) for a in arrays]


def scores_kernel(first, scal, diag, xa, xb, ta, tb, *refs):
    before = refs[:1] if len(refs) == 5 else ()
    wgt, out_sums, sim, sums = refs[-4:]
    scores(scal, diag, first, (xa, xb), (ta, tb), sim, wgt, sums)
    if before:
        total = sums[...] + before[0][...]
        lane = lax.broadcasted_iota(jnp.int32, (8, 128), 1)
        out = jnp.zeros((8, 128), F32)
        for k in range(3):
            out = jnp.where(lane == k, jnp.sum(total[8 * k : 8 * k + 8], keepdims=True), out)
        out_sums[...] = out[0:1]
    else:
        out_sums[...] = sums[...]


def score_half(first, scal, diag, images, texts, before=()):
    d = images[0].shape[1]
    m = n = 2 * images[0].shape[0]
    return pl.pallas_call(
        lambda *refs: scores_kernel(first, *refs),
        in_specs=[SM, SM] + [VM] * (4 + len(before)),
        out_specs=[VM, VM],
        out_shape=(sds((m, n), BF), sds((1, 128) if before else (24, PIECE), F32)),
        scratch_shapes=[pltpu.VMEM((m, n), F32), pltpu.VMEM((24, PIECE), F32)],
        compiler_params=params(),
        cost_estimate=pl.CostEstimate(
            flops=2 * m * n * d, bytes_accessed=(m + n) * d * 2, transcendentals=3 * m * n
        ),
        name="scores",
    )(scal, diag, *here(*images, *texts, *before))


def group_pull(dims, k, weights, pairs):
    total = None
    for w, pair in zip(weights, pairs):
        tall = pair[0].shape[0]
        rows = tall // 4
        one, two = (slice(b * rows, (b + 1) * rows) for b in GROUP[k])
        for h, r in enumerate(pair):
            at = slice(h * tall, (h + 1) * tall)
            if dims == 1:
                lhs = jnp.concatenate([w[one, at], w[two, at]], 0)
            else:
                lhs = jnp.concatenate([w[at, one], w[at, two]], 1)
            part = dot(lhs, r[...], ((dims,), (0,)))
            total = part if total is None else total + part
    return total


def put_row(ref, at, row):
    zero = jnp.zeros((16, ref.shape[1] - 384), BF)
    for n in range(3):
        part = row.astype(BF)
        row = row - part.astype(F32)
        ref[at : at + 16, 128 * n : 128 * n + 128] = jnp.broadcast_to(part.astype(F32), (16, 128)).astype(BF)
    ref[at : at + 16, 384:] = zero


def get_row(ref, at):
    part = [ref[at : at + 16, 128 * n : 128 * n + 128].astype(F32)[0:1] for n in range(3)]
    return (part[0] + part[1]) + part[2]


def far_kernel(dims, w0, w1, r0a, r0b, r1a, r1b, *refs):
    out_a, out_b = refs[-2:]
    total = group_pull(dims, 2, (w0, w1), ((r0a, r0b), (r1a, r1b)))
    rows = total.shape[0] // 2
    for out, half in ((out_a, total[:rows]), (out_b, total[rows:])):
        out[:rows, :] = encode(half)
        if len(refs) == 3:
            put_row(out, rows, refs[0][...])


def near_kernel(dims, w0, w1, r0a, r0b, r1a, r1b, via_a, via_b, o1, o3, own, *sides):
    rows = own.shape[0] // 2
    for k, out in ((1, o1), (3, o3), (0, own)):
        total = group_pull(dims, k, (w0, w1), ((r0a, r0b), (r1a, r1b)))
        one, two = total[:rows], total[rows:]
        if k == 0:
            out[...] = total
            continue
        if k == 1:
            two = two + decode(via_b[:rows, :])
        else:
            one = one + decode(via_a[:rows, :])
        out[:rows, :] = encode(one)
        out[rows : 2 * rows, :] = encode(two)
    if sides:
        o1[2 * rows :, :] = via_b[rows:, :]
        sides[0][...] = get_row(via_a, rows) + get_row(via_b, rows)


def pulls(dims, w0, w1, rows0, rows1, name, via=(), row=()):
    rows, d = rows0[0].shape[0] // 4, rows0[0].shape[1]
    n = w0.shape[dims]
    if via:
        more = via[0].shape[0] - rows
        shapes = [sds((2 * rows + more, d), BF), sds((2 * rows, d), BF), sds((2 * rows, d), F32)]
        shapes += [sds((1, 128), F32)] if more else []
    else:
        shapes = [sds((rows + 16 * len(row), d), BF)] * 2
    return pl.pallas_call(
        functools.partial(near_kernel if via else far_kernel, dims),
        in_specs=[VM] * (6 + len(via) + len(row)),
        out_specs=[VM] * len(shapes),
        out_shape=shapes,
        compiler_params=params(),
        cost_estimate=pl.CostEstimate(
            flops=8 * (3 if via else 1) * rows * n * d, bytes_accessed=4 * n * d, transcendentals=0
        ),
        name=name,
    )(*here(w0, w1, *rows0, *rows1, *via, *row))


def image_partner_kernel(own, c1, c3, v, sides, out, v_out):
    partner_kernel(own, c1, c3, out)
    v_out[...] = (v[...] + get_row(c1, own.shape[0])) + sides[...]


def fold_image_partner(own, codes, v, sides):
    rows, d = own.shape[0] // 2, own.shape[1]
    return pl.pallas_call(
        image_partner_kernel,
        in_specs=[VM] * 5,
        out_specs=[VM] * 2,
        out_shape=(sds((rows, d), BF), sds((1, 128), F32)),
        compiler_params=small(),
        name="fold_image_partner",
    )(*here(own, *codes, v, sides))


def partner_kernel(own, c1, c3, out):
    at = pl.ds(out.shape[0], out.shape[0])
    out[...] = encode(own[at, :] + decode(c1[at, :]) + decode(c3[at, :]))


def own_kernel(own, c1, c3, out):
    at = pl.ds(0, out.shape[0])
    out[...] = own[at, :] + decode(c1[at, :]) + decode(c3[at, :])


def fold(kernel, own, codes, dtype, name):
    rows, d = own.shape[0] // 2, own.shape[1]
    return pl.pallas_call(
        kernel,
        in_specs=[VM] * 3,
        out_specs=VM,
        out_shape=sds((rows, d), dtype),
        compiler_params=small(),
        name=name,
    )(*here(own, *codes))


def finish_kernel(hat_ref, norm_ref, own, code_ref, out_ref):
    hat = hat_ref[...]
    pull = own[...] + decode(code_ref[...])
    out_ref[...] = (pull - hat * jnp.sum(hat * pull, axis=1, keepdims=True)) / norm_ref[...]


def finish(hat, norm, own, code):
    return pl.pallas_call(
        finish_kernel,
        in_specs=[VM] * 4,
        out_specs=VM,
        out_shape=sds(hat.shape, F32),
        compiler_params=small(),
        name="finish",
    )(*here(hat, norm, own, code))


def img_index(y, z, c):
    return (y % 4) * 4 + (z % 2) * 2 + c % 2


def perm_x(shift):
    return [(i, ((i // 2 + shift) % 4) * 2 + i % 2) for i in range(8)]


def perm_y(shift):
    return [(i, img_index(i // 4 + shift, i // 2, i)) for i in range(16)]


PERM_ZHI = [(i, i ^ 1) for i in range(8)]
PERM_ZLO = [(i, i ^ 2) for i in range(16)]
PERM_CORE = [(i, i ^ 1) for i in range(16)]
send = lax.ppermute


def after(x, *others):
    return lax.optimization_barrier((x, *others))[0]


def gather(image, text):
    ways = ((image, "txt", perm_x, PERM_ZHI), (text, "img", perm_y, PERM_ZLO))
    z = [send(low, axis, pz) for low, axis, _, pz in ways]
    a1 = [send(low, axis, perm(1)) for low, axis, perm, _ in ways]
    a3 = [send(low, axis, perm(-1)) for low, axis, perm, _ in ways]
    a2 = [send(a, axis, perm(1)) for a, (_, axis, perm, _) in zip(a1, ways)]
    z, a1, a3, a2 = lax.optimization_barrier((z, a1, a3, a2))
    z3 = [send(b, axis, perm(-1)) for b, (_, axis, perm, _) in zip(z, ways)]
    z1 = [send(b, axis, perm(1)) for b, (_, axis, perm, _) in zip(z, ways)]
    z3, z1 = lax.optimization_barrier((z3, z1))
    z2 = lax.optimization_barrier([send(b, axis, perm(-1)) for b, (_, axis, perm, _) in zip(z3, ways)])
    return [
        (jnp.concatenate([w[0], a1[n], a3[n], a2[n]], 0), jnp.concatenate([z[n], z1[n], z3[n], z2[n]], 0))
        for n, w in enumerate(ways)
    ]


def exchange_sum(v, axis, *perms):
    got = [send(v, a, p) for a, p in zip(axis, perms)]
    return v + got[0] if len(got) == 1 else (v + got[1]) + (got[0] + got[2])


def local(image_embed, text_embed, log_scale, logit_bias):
    rows, d = image_embed.shape
    (image_low, image_hat, image_norm), (text_low, text_hat, text_norm) = normalize(image_embed, text_embed)
    images, own = gather(image_low, text_low)
    other = [send(t, "img", PERM_CORE) for t in own]
    partner = [send(x, "img", PERM_CORE) for x in images]

    i, t = lax.axis_index("img"), lax.axis_index("txt")
    ring, zz = jnp.array(RING, jnp.int32), jnp.array(PARTNER, jnp.int32)
    g = 8 * i + ((t // 2 - ring) % 4) * 2 + ((t % 2) ^ zz)
    o = g % 16
    k, z = (i // 4 - o // 4) % 4, ((i // 2) % 2) ^ ((o // 2) % 2)
    mine = 1 - ((i % 2) ^ (o % 2))
    found = jnp.logical_and(k[:, None] == ring[None, :], z[:, None] == zz[None, :])
    place = mine * 8 + jnp.sum(jnp.where(found, jnp.arange(8, dtype=jnp.int32)[None, :], 0), 1)
    diag = jnp.where(g // 16 == t, place, -1).astype(jnp.int32)
    scale = jnp.exp(log_scale)
    scal = jnp.stack([scale, logit_bias, scale * LOG2E, logit_bias * LOG2E])

    w_own, sums = score_half(8, scal, diag, images, own)
    w_oth, v = score_half(0, scal, diag, images, other, (sums,))
    w_rec = send(w_oth, "img", PERM_CORE)

    ia, ib = pulls(1, w_own, w_oth, own, other, "far_image", row=(v,))
    ia, ib = send(ia, "txt", perm_x(1)), send(ib, "txt", perm_x(-1))
    ta, tb = pulls(0, w_own, w_rec, images, partner, "far_text")
    ta, tb = send(ta, "img", perm_y(1)), send(tb, "img", perm_y(-1))
    i1, i3, i0, sides = pulls(1, w_own, w_oth, own, other, "near_image", (ia, ib))
    i1, i3 = send(i1, "txt", perm_x(-1)), send(i3, "txt", perm_x(1))
    t1, t3, t0 = pulls(0, after(w_own, i0), w_rec, images, partner, "near_text", (ta, tb))
    t1, t3 = send(t1, "img", perm_y(-1)), send(t3, "img", perm_y(1))

    image_code, v = fold_image_partner(i0, (i1, i3), v, sides)
    image_code = send(image_code, "txt", PERM_ZHI)
    image_own = fold(own_kernel, i0, (i1, i3), F32, "fold_own")
    v = exchange_sum(v, ("img",), PERM_CORE)
    text_code = fold(partner_kernel, t0, (t1, t3), BF, "fold_partner")
    v = after(v, text_code)
    both = [(n, n ^ 17) for n in range(128)]
    v = exchange_sum(v, ("img", ("img", "txt"), "txt"), PERM_ZLO, both, PERM_ZHI)
    text_code = send(text_code, "img", PERM_ZLO)
    text_own = fold(own_kernel, t0, (t1, t3), F32, "fold_own")
    v = exchange_sum(v, ("img",) * 3, perm_y(1), perm_y(2), perm_y(-1))
    image_grad = finish(image_hat, image_norm, image_own, image_code)
    text_grad = finish(text_hat, text_norm, after(text_own, v), text_code)
    pairs = F32(128.0 * rows) * F32(128.0 * rows)
    return (v[0, 0] / pairs, image_grad, text_grad, v[0, 2] * scale / pairs, v[0, 1] / pairs)


def solution(mesh):
    placed = (P(("img", "txt"), None), P(("txt", "img"), None), P(), P())
    return jax.shard_map(
        local,
        mesh=mesh,
        in_specs=placed,
        out_specs=(P(), P(("img", "txt"), None), P(("txt", "img"), None), P(), P()),
        check_vma=False,
    )
```
